256 devices in a mesh: level: 2 (over x_lo), row: 16 (over z, core), col: 8 (over y, x_hi).
Axes of the slice: x: 4 (x_hi: 2, x_lo: 2; x = x_hi * 2 + x_lo), y: 4, z: 8, core: 2. Of those that a mesh axis runs over, the one named last changes fastest.
Arguments:
- noise: bfloat16 [64, 512, 512], P('row', ('level', 'col')), may hold values from -6 to 6
- source: bfloat16 [64, 512, 512], P('row', ('level', 'col')), may hold values from -16 to 16
Outputs:
- fine_pressure: float32 [64, 512, 512], P('row', ('level', 'col'))
- coarse_pressure: float32 [32, 256, 256], P('row', ('level', 'col'))
The draws below stay inside these ranges and needn't reach their ends.
All inputs are finite; a program needn't handle non-finite values.
Results may differ from the reference program's by a relative error of at most 0.00035.
Values sent between devices are 32-bit elements; how exact they have to be, the bound alone decides.
A program may use at most 128 MiB of HBM per device.

```python
import math
import jax
import jax.numpy as jnp

NF = 512
NZ = 64
NC = 256
NCZ = 32


def levels(stream_key, shape, pieces, low, largest):
    loudness, own = 1.0, jax.random.fold_in(stream_key, 6)
    for dim, blocks in pieces:
        draws = jnp.exp(jax.random.uniform(jax.random.fold_in(own, dim), (blocks,), jnp.float32, low / len(pieces), largest / len(pieces)))
        loudness = loudness * jnp.repeat(draws, shape[dim] // blocks).reshape([-1 if axis == dim else 1 for axis in range(len(shape))])
    return loudness


def scatter_about(stream_key, shape, width, reach, pieces=(), held_as=jnp.bfloat16):
    loudness = levels(stream_key, shape, pieces, -0.22, 0.18) if pieces else 1.0
    array = jax.random.normal(stream_key, shape, jnp.float32) * width * loudness
    return jnp.minimum(jnp.maximum(array, -reach), reach).astype(held_as)


def setup_inputs(seed: int = 0) -> dict:
    key_list = jax.random.split(jax.random.key(seed), 3)
    return {
        "noise": scatter_about(key_list[0], (NZ, NF, NF), 1.0, 6.0, ((0, 16), (1, 16))),
        "source": scatter_about(key_list[1], (NZ, NF, NF), 4.0, 16.0, ((0, 16), (1, 16))),
    }


JACOBI_WEIGHT = 2.0 / 3.0
CORRELATION = 0.2
FIELD_SCALE = 0.3
NEIGHBOUR_STEPS = ((1, 0, 0), (-1, 0, 0), (0, 1, 0), (0, -1, 0), (0, 0, 1), (0, 0, -1))


def signed_modes(index, length):
    return jnp.where(index < length // 2, index, index - length).astype(jnp.float32)


def amplitude(first_modes, second_modes, third_modes, first_edge, second_edge, third_edge):
    squared = first_modes * first_modes + second_modes * second_modes + third_modes * third_modes
    value = FIELD_SCALE / (1.0 + (2.0 * math.pi * CORRELATION) ** 2 * squared)
    edge = (jnp.abs(first_modes) == first_edge) | (jnp.abs(second_modes) == second_edge) | (jnp.abs(third_modes) == third_edge)
    return jnp.where(edge, 0.0, value)


def window(values, margin, offset):
    return values[margin + offset[0]: values.shape[0] - margin + offset[0],
                  margin + offset[1]: values.shape[1] - margin + offset[1],
                  margin + offset[2]: values.shape[2] - margin + offset[2]]


def face_weight(center, beside):
    return jnp.where(beside > 0.0, 0.5 * (center + beside), center)


def smooth_twice(kappa, source):
    no_shift = (0, 0, 0)
    center = window(kappa, 1, no_shift)
    faces = [face_weight(center, window(kappa, 1, offset)) for offset in NEIGHBOUR_STEPS]
    diagonal = faces[0] + faces[1] + faces[2] + faces[3] + faces[4] + faces[5]
    guarded = jnp.where(center > 0.0, diagonal, 1.0)
    first_sweep = JACOBI_WEIGHT * window(source, 1, no_shift) / guarded
    inner_first = window(first_sweep, 1, no_shift)
    inner_diagonal = window(diagonal, 1, no_shift)
    coupled = jnp.zeros_like(inner_first)
    for face_value, offset in zip(faces, NEIGHBOUR_STEPS):
        coupled = coupled + window(face_value, 1, no_shift) * window(first_sweep, 1, offset)
    residual = window(source, 2, no_shift) - inner_diagonal * inner_first + coupled
    return inner_first + JACOBI_WEIGHT * residual / inner_diagonal


def reference(noise, source):
    field = noise.astype(jnp.float32)
    spectrum = jnp.fft.rfftn(field)
    total_cells = float(NZ) * float(NF) * float(NF)
    slab_modes = signed_modes(jnp.arange(NZ, dtype=jnp.int32), NZ)
    fine_modes = signed_modes(jnp.arange(NF, dtype=jnp.int32), NF)
    third_fine = jnp.arange(NF // 2 + 1, dtype=jnp.int32).astype(jnp.float32)
    fine_scale = amplitude(slab_modes[:, None, None], fine_modes[None, :, None], third_fine[None, None, :], NZ / 2.0, NF / 2.0, NF / 2.0)
    fine_log = jnp.fft.irfftn(spectrum * fine_scale, s=(NZ, NF, NF)) * (total_cells ** 0.5)
    half_slab = NCZ // 2
    half_coarse = NC // 2
    band = jnp.concatenate([spectrum[:half_slab], spectrum[NZ - half_slab:]], axis=0)
    band = jnp.concatenate([band[:, :half_coarse], band[:, NF - half_coarse:]], axis=1)
    band = band[:, :, :half_coarse + 1]
    coarse_slab_modes = signed_modes(jnp.arange(NCZ, dtype=jnp.int32), NCZ)
    coarse_modes = signed_modes(jnp.arange(NC, dtype=jnp.int32), NC)
    third_coarse = jnp.arange(half_coarse + 1, dtype=jnp.int32).astype(jnp.float32)
    coarse_scale = amplitude(coarse_slab_modes[:, None, None], coarse_modes[None, :, None], third_coarse[None, None, :], NCZ / 2.0, NC / 2.0, NC / 2.0)
    coarse_cells = float(NCZ) * float(NC) * float(NC)
    coarse_log = jnp.fft.irfftn(band * coarse_scale, s=(NCZ, NC, NC)) * (coarse_cells / total_cells ** 0.5)
    fine_source = source.astype(jnp.float32)
    coarse_source = fine_source.reshape(NCZ, 2, NC, 2, NC, 2).mean(axis=(1, 3, 5))
    fine_pressure = smooth_twice(jnp.pad(jnp.exp(fine_log), 2), jnp.pad(fine_source, 2))
    coarse_pressure = smooth_twice(jnp.pad(jnp.exp(coarse_log), 2), jnp.pad(coarse_source, 2))
    return fine_pressure, coarse_pressure
```

```python
import functools
import math

import jax
import jax.numpy as jnp
import ml_dtypes
import numpy as np
from jax import lax
from jax.experimental import pallas as pl
from jax.experimental.pallas import tpu as pltpu
from jax.sharding import PartitionSpec as P

JACOBI_WEIGHT = 2.0 / 3.0
CORRELATION = 0.2
FIELD_SCALE = 0.3
LOGICAL = pl.DeviceIdType.LOGICAL
F32 = jnp.float32
BF16 = jnp.bfloat16

N0, N1, N2 = 64, 512, 512
ROWS, COLS = 16, 16
DEVICES = ROWS * COLS
PB, QB = N0 // ROWS, N1 // COLS
LANES = PB * QB
EDGE = 8


def split_table(table):
    high = table.astype(ml_dtypes.bfloat16)
    low = (table - high.astype(np.float64)).astype(ml_dtypes.bfloat16)
    return high, low


def signed(index, length):
    return np.where(index < length // 2, index, index - length).astype(np.float64)


@functools.lru_cache(maxsize=None)
def tables():
    place = np.arange(DEVICES)
    r, c = place // COLS, place % COLS
    third = (r % 2) * 128 + (r // 2) * 16 + c
    turn = 2.0 * np.pi
    n2 = np.arange(N2)
    angle = turn * ((third[:, None] * n2[None, :]) % N2) / N2
    third_table = np.stack([np.cos(angle), -np.sin(angle)], axis=1).reshape(2 * DEVICES, N2)
    k2 = np.arange(128)
    angle = turn * ((k2[:, None] * np.arange(N2 // 2)[None, :]) % (N2 // 2)) / (N2 // 2)
    coarse_third = np.concatenate([np.cos(angle), -np.sin(angle)], axis=0)
    a, b = place // 16, place % 16
    angle = turn * ((a[:, None] * r[None, :] + b[:, None] * c[None, :]) % 16) / 16
    cos, sin = np.cos(angle), np.sin(angle)
    outer = np.concatenate([np.stack([cos, sin], axis=2), np.stack([-sin, cos], axis=2)], axis=0)
    outer = outer.reshape(2 * DEVICES, 2 * DEVICES)
    lane = np.arange(LANES)
    p, q = lane // QB, lane % QB
    angle = turn * (((8 * p[:, None] * p[None, :]) + q[:, None] * q[None, :]) % 32) / 32
    cos, sin = np.cos(angle), np.sin(angle)
    inner = np.block([[cos, -sin], [sin, cos]])
    lane_c = np.arange(32)
    pc, qc = lane_c // 16, lane_c % 16
    angle = turn * (((8 * p[:, None] * pc[None, :]) + q[:, None] * qc[None, :]) % 16) / 16
    cos, sin = np.cos(angle), np.sin(angle)
    empty = np.zeros((LANES, LANES - 64))
    inner_c = np.block([[cos, cos, empty, sin, sin, empty], [-sin, -sin, empty, cos, cos, empty]])
    angle = turn * ((8 * a[:, None] * p[None, :] + b[:, None] * q[None, :]) % 512) / 512
    twist = np.stack([np.cos(angle), np.sin(angle)])
    angle = turn * ((8 * a[:, None] * pc[None, :] + b[:, None] * qc[None, :]) % 256) / 256
    cos, sin = np.cos(angle), np.sin(angle)
    rest = np.zeros((DEVICES, LANES - 64))
    twist_c = np.stack([np.concatenate([cos, sin, rest], 1), np.concatenate([sin, -cos, rest], 1)])
    m0 = signed(a[:, None] + 16 * p[None, :], N0)
    m1 = signed(b[:, None] + 16 * q[None, :], N1)
    norm = (float(N0) * N1 * N2) ** -0.5
    inside = (m0 != -N0 // 2) & (m1 != -N1 // 2)
    inside_c = (np.abs(m0) < N0 // 4) & (np.abs(m1) < N1 // 4)
    waves = np.stack([m0 * m0 + m1 * m1, inside * FIELD_SCALE * norm, inside_c * FIELD_SCALE * norm])
    pool = (np.arange(N2)[:, None] // 2 == np.arange(N2 // 2)[None, :]).astype(ml_dtypes.bfloat16)
    pool_rows = (lane_c[:, None] == ((p // 2) * 16 + q // 2)[None, :]) * 0.125
    return (
        np.stack(split_table(third_table)),
        np.stack(split_table(outer)),
        np.stack(split_table(outer.T)),
        np.stack(split_table(inner)),
        np.stack(split_table(inner.T)),
        np.stack(split_table(inner_c)),
        np.stack(split_table(coarse_third)),
        pool,
        pool_rows.astype(ml_dtypes.bfloat16),
        twist.astype(np.float32),
        twist_c.astype(np.float32),
        waves.astype(np.float32),
    )


def halves(value):
    high = value.astype(BF16)
    return high, (value - high.astype(F32)).astype(BF16)


def dot(left, right):
    return jnp.dot(left, right, preferred_element_type=F32)


def table_left(table, value):
    high, low = halves(value)
    width = value.shape[1]
    both = dot(table[0], jnp.concatenate([high, low], axis=1))
    return both[:, :width] + (both[:, width:] + dot(table[1], high))


def table_right(value, table):
    high, low = halves(value)
    return dot(high, table[0]) + (dot(high, table[1]) + dot(low, table[0]))


DIRECTIONS = ((-1, 0), (1, 0), (0, -1), (0, 1), (-1, -1), (-1, 1), (1, -1), (1, 1))
OPPOSITE = (1, 0, 3, 2, 7, 6, 5, 4)


def flat_id(r, c):
    return (c // 8) * 128 + r * 8 + c % 8


def face_weight(center, beside):
    return jnp.where(beside > 0.0, 0.5 * (center + beside), center)


def smooth(kappa, source, first, out, planes, width, depth):
    tall = width + 2 * EDGE
    lane = lax.broadcasted_iota(jnp.int32, (tall, depth), 1)
    lane_in = lax.broadcasted_iota(jnp.int32, (width, depth), 1)
    diagonals = []
    for plane in range(planes + 2):
        center = kappa[plane + 1]
        diagonal = face_weight(center, kappa[plane + 2])
        diagonal = diagonal + face_weight(center, kappa[plane])
        diagonal = diagonal + face_weight(center, pltpu.roll(center, tall - 1, 0))
        diagonal = diagonal + face_weight(center, pltpu.roll(center, 1, 0))
        after = jnp.where(lane == depth - 1, 0.0, pltpu.roll(center, depth - 1, 1))
        before = jnp.where(lane == 0, 0.0, pltpu.roll(center, 1, 1))
        diagonal = diagonal + face_weight(center, after) + face_weight(center, before)
        guarded = jnp.where(center > 0.0, diagonal, 1.0)
        first[plane] = JACOBI_WEIGHT * source[plane] / guarded
    mid, low, high = pl.ds(EDGE, width), pl.ds(EDGE - 1, width), pl.ds(EDGE + 1, width)
    for plane in range(planes):
        center = kappa[plane + 2, mid]
        inner = first[plane + 1, mid]
        total = jnp.zeros_like(center)
        diagonal = jnp.zeros_like(center)
        for beside, value in (
            (kappa[plane + 3, mid], first[plane + 2, mid]),
            (kappa[plane + 1, mid], first[plane, mid]),
            (kappa[plane + 2, high], first[plane + 1, high]),
            (kappa[plane + 2, low], first[plane + 1, low]),
        ):
            face = face_weight(center, beside)
            diagonal = diagonal + face
            total = total + face * value
        for shift, missing in ((depth - 1, depth - 1), (1, 0)):
            outside = lane_in == missing
            beside = jnp.where(outside, 0.0, pltpu.roll(center, shift, 1))
            value = jnp.where(outside, 0.0, pltpu.roll(inner, shift, 1))
            face = face_weight(center, beside)
            diagonal = diagonal + face
            total = total + face * value
        residual = source[plane + 1, mid] - diagonal * inner + total
        out[plane] = inner + JACOBI_WEIGHT * residual / diagonal


def kernel(
    noise, source, third_h, outer_h, outer_t_h, inner_h, inner_t_h, inner_c_h, coarse_third_h, pool_h, pool_rows_h, twist_h, twist_c_h,
    waves_h, fine_out, coarse_out,
    third_t, outer, outer_t, inner, inner_t, inner_c, coarse_third, pool, pool_rows, twist, twist_c, waves,
    send_f, recv_f, send_i, recv_i, send_c, recv_c,
    ke, fe, ue, kc, fc, uc,
    col_s, col_r, ccol_s, ccol_r, cor_s, cor_r, ccor_s, ccor_r, scol_s, scol_r, cscol_s, cscol_r,
    table_sem, fwd_sem, inv_sem, crs_sem, own_sem, halo_s, halo_r, chalo_s, chalo_r, src_s, src_r, csrc_s, csrc_r,
):
    level, row, col = lax.axis_index("level"), lax.axis_index("row"), lax.axis_index("col")
    group = level * 8 + col
    me = flat_id(row, group)
    place = row * COLS + group
    core = row % 2

    for ref in (ke, fe, kc, fc):
        ref[...] = jnp.zeros_like(ref)

    barrier = pltpu.get_barrier_semaphore()

    def greet(i, carry):
        pl.semaphore_signal(barrier, inc=1, device_id=(me + i) % DEVICES, device_id_type=LOGICAL)
        return carry

    lax.fori_loop(1, DEVICES, greet, 0, unroll=15)

    pairs = (
        (third_h, third_t), (pool_h, pool), (pool_rows_h, pool_rows), (outer_h, outer), (twist_h, twist), (inner_h, inner), (waves_h, waves),
        (inner_t_h, inner_t), (inner_c_h, inner_c), (twist_c_h, twist_c), (outer_t_h, outer_t),
        (coarse_third_h, coarse_third),
    )
    loads = [pltpu.make_async_copy(a, b, table_sem.at[i]) for i, (a, b) in enumerate(pairs)]
    for load in loads:
        load.start()

    fe[pl.ds(1, PB), pl.ds(EDGE, QB)] = source[...].astype(F32)
    scol_s[0, :, 0] = source[:, 0].astype(F32)
    scol_s[1, :, 0] = source[:, QB - 1].astype(F32)
    loads[0].wait()
    noise_rows = noise[...].reshape(LANES, N2)
    contract = (((1,), (1,)), ((), ()))
    spectrum = lax.dot_general(third_t[0], noise_rows, contract, preferred_element_type=F32)
    spectrum = spectrum + lax.dot_general(third_t[1], noise_rows, contract, preferred_element_type=F32)
    send_f[...] = spectrum.reshape(DEVICES, 2, LANES)
    loads[1].wait()
    loads[2].wait()
    high, low = halves(dot(pool_rows[...], source[...].reshape(LANES, N2)))
    pooled = (dot(high, pool[...]) + dot(low, pool[...])).reshape(PB // 2, QB // 2, N2 // 2)
    fc[pl.ds(1, PB // 2), pl.ds(EDGE, QB // 2)] = pooled
    cscol_s[0, :, 0] = pooled[:, 0]
    cscol_s[1, :, 0] = pooled[:, QB // 2 - 1]

    pl.semaphore_wait(barrier, DEVICES - 1)

    def peer_at(i):
        j = i // 32
        half = (j + 1) // 2
        z = (row // 2 + 4 + jnp.where(j % 2 == 1, -half, half)) % 8
        k = 31 - i % 32
        r = z * 2 + (core + k // 16) % 2
        y = (col // 2 + (k // 4) % 4) % 4
        x = ((col % 2) * 2 + level + k % 4) % 4
        c = (x % 2) * 8 + y * 2 + x // 2
        return r, c

    def push(i, carry):
        r, c = peer_at(i)
        pltpu.make_async_remote_copy(
            src_ref=send_f.at[r * COLS + c], dst_ref=recv_f.at[place], send_sem=fwd_sem.at[0], recv_sem=fwd_sem.at[1],
            device_id=flat_id(r, c), device_id_type=LOGICAL,
        ).start()
        return carry

    lax.fori_loop(0, DEVICES - 1, push, 0, unroll=15)
    recv_f[place] = send_f[place]

    def neighbour(d):
        dr, dc = DIRECTIONS[d]
        r, c = row + dr, group + dc
        exists = (r >= 0) & (r < ROWS) & (c >= 0) & (c < COLS)
        return exists, flat_id(r, c)

    def halo_copies(d, kind):
        half_p, half_q = PB // 2, QB // 2
        mid, mid_c = pl.ds(EDGE, QB), pl.ds(EDGE, half_q)
        back = OPPOSITE[d]
        if kind == "source":
            if d < 2:
                here = (fe.at[1 if d == 0 else PB, mid], fe.at[PB + 1 if d == 0 else 0, mid], fe.at[0 if d == 0 else PB + 1, mid])
                there = (
                    fc.at[1 if d == 0 else half_p, mid_c], fc.at[half_p + 1 if d == 0 else 0, mid_c],
                    fc.at[0 if d == 0 else half_p + 1, mid_c],
                )
                return ((*here, src_s, src_r), (*there, csrc_s, csrc_r))
            return (
                (scol_s.at[d - 2], scol_r.at[back - 2], scol_r.at[d - 2], src_s, src_r),
                (cscol_s.at[d - 2], cscol_r.at[back - 2], cscol_r.at[d - 2], csrc_s, csrc_r),
            )
        if d < 2:
            return (
                (
                    ke.at[pl.ds(2 if d == 0 else PB, 2), mid], ke.at[pl.ds(PB + 2 if d == 0 else 0, 2), mid],
                    ke.at[pl.ds(0 if d == 0 else PB + 2, 2), mid], halo_s, halo_r,
                ),
                (
                    kc.at[pl.ds(2, 2), mid_c], kc.at[pl.ds(half_p + 2 if d == 0 else 0, 2), mid_c],
                    kc.at[pl.ds(0 if d == 0 else half_p + 2, 2), mid_c], chalo_s, chalo_r,
                ),
            )
        if d < 4:
            return (
                (col_s.at[d - 2], col_r.at[back - 2], col_r.at[d - 2], halo_s, halo_r),
                (ccol_s.at[d - 2], ccol_r.at[back - 2], ccol_r.at[d - 2], chalo_s, chalo_r),
            )
        return (
            (cor_s.at[d - 4], cor_r.at[back - 4], cor_r.at[d - 4], halo_s, halo_r),
            (ccor_s.at[d - 4], ccor_r.at[back - 4], ccor_r.at[d - 4], chalo_s, chalo_r),
        )

    def halo_start(d, kind, which):
        exists, there = neighbour(d)
        src, dst, _, s_sem, r_sem = halo_copies(d, kind)[which]

        @pl.when(exists)
        def _():
            pltpu.make_async_remote_copy(
                src_ref=src, dst_ref=dst, send_sem=s_sem.at[d], recv_sem=r_sem.at[OPPOSITE[d]], device_id=there,
                device_id_type=LOGICAL,
            ).start()

    def halo_wait(d, kind, which, then):
        exists, there = neighbour(d)
        src, _, here, s_sem, r_sem = halo_copies(d, kind)[which]

        @pl.when(exists)
        def _():
            copy = pltpu.make_async_remote_copy(
                src_ref=src, dst_ref=here, send_sem=s_sem.at[d], recv_sem=r_sem.at[d], device_id=there,
                device_id_type=LOGICAL,
            )
            copy.wait_send()
            copy.wait_recv()
            if then is not None:
                then()

    for d in range(4):
        for which in range(2):
            halo_start(d, "source", which)
    for load in loads[3:]:
        load.wait()

    many = pl.ds(0, DEVICES - 1)
    arrived = pltpu.make_async_remote_copy(
        src_ref=send_f.at[many], dst_ref=recv_f.at[many], send_sem=fwd_sem.at[0], recv_sem=fwd_sem.at[1], device_id=me,
        device_id_type=LOGICAL,
    )
    arrived.wait_recv()

    z = table_left(outer, recv_f[...].reshape(2 * DEVICES, LANES))
    z_re, z_im = z[:DEVICES], z[DEVICES:]
    turned = jnp.concatenate([z_re * twist[0] + z_im * twist[1], z_im * twist[0] - z_re * twist[1]], axis=1)
    y = table_right(turned, inner)
    third = core * 128 + (row // 2) * 16 + group
    third_f = third.astype(F32)
    weight = jnp.where(third == 0, 1.0, 2.0)
    damp = weight / (1.0 + (2.0 * math.pi * CORRELATION) ** 2 * (waves[0] + third_f * third_f))
    amp = waves[1] * damp
    amp_c = waves[2] * damp
    x = table_right(y * jnp.concatenate([amp, amp], axis=1), inner_t)
    x_re, x_im = x[:, :LANES], x[:, LANES:]
    xc = table_right(y * jnp.concatenate([amp_c, amp_c], axis=1), inner_c)
    xc_re, xc_im = xc[:, :LANES], xc[:, LANES:]
    fine_part = jnp.concatenate([x_re * twist[0] - x_im * twist[1], x_im * twist[0] + x_re * twist[1]], axis=0)
    coarse_part = jnp.concatenate(
        [xc_re * twist_c[0] - xc_im * twist_c[1], xc_im * twist_c[0] + xc_re * twist_c[1]], axis=0
    )
    both = jnp.concatenate([fine_part, coarse_part], axis=1)
    high, low = halves(both)
    planes = dot(outer_t[0], high) + (dot(outer_t[0], low) + dot(outer_t[1], high))
    send_i[...] = planes[:, :LANES].reshape(DEVICES, 2, LANES)
    send_c[...] = planes[:, LANES:].reshape(DEVICES, 2, LANES)[:, 0:1, :]

    def push_back(i, carry):
        r, c = peer_at(i)
        pltpu.make_async_remote_copy(
            src_ref=send_i.at[r * COLS + c], dst_ref=recv_i.at[place], send_sem=inv_sem.at[0], recv_sem=inv_sem.at[1],
            device_id=flat_id(r, c), device_id_type=LOGICAL,
        ).start()
        return carry

    def push_coarse(i, carry):
        r, c = peer_at(i)
        pltpu.make_async_remote_copy(
            src_ref=send_c.at[r * COLS + c], dst_ref=recv_c.at[(row // 2) * COLS + group], send_sem=crs_sem.at[0],
            recv_sem=crs_sem.at[1], device_id=flat_id(r, c), device_id_type=LOGICAL,
        ).start()
        return carry

    lax.fori_loop(0, DEVICES - 1, push_back, 0, unroll=15)
    recv_i[place] = send_i[place]

    @pl.when(core == 0)
    def _():
        lax.fori_loop(0, DEVICES - 1, push_coarse, 0, unroll=15)
        recv_c[(row // 2) * COLS + group] = send_c[place]

    back = pltpu.make_async_remote_copy(
        src_ref=send_i.at[many], dst_ref=recv_i.at[many], send_sem=inv_sem.at[0], recv_sem=inv_sem.at[1], device_id=me,
        device_id_type=LOGICAL,
    )
    back.wait_recv()
    field = recv_i[...].reshape(2 * DEVICES, LANES)
    fine_log = table_right(field.T, third_t)
    fine_kappa = jnp.exp(fine_log).reshape(PB, QB, N2)
    ke[pl.ds(2, PB), pl.ds(EDGE, QB)] = fine_kappa
    for d in range(2):
        halo_start(d, "kappa", 0)
    col_s[0] = fine_kappa[:, 0:2]
    col_s[1] = fine_kappa[:, QB - 2 : QB]
    for i, (dr, dc) in enumerate(DIRECTIONS[4:]):
        cor_s[i, 0] = fine_kappa[0 if dr < 0 else PB - 1, 0 if dc < 0 else QB - 1]
    for d in range(2, 8):
        halo_start(d, "kappa", 0)

    @pl.when(core == 0)
    def _():
        mine = pl.ds(0, 127)
        pltpu.make_async_remote_copy(
            src_ref=recv_c.at[mine], dst_ref=recv_c.at[mine], send_sem=crs_sem.at[0], recv_sem=crs_sem.at[1],
            device_id=me, device_id_type=LOGICAL,
        ).wait_recv()

    @pl.when(core == 1)
    def _():
        mine = pl.ds(0, 128)
        pltpu.make_async_remote_copy(
            src_ref=recv_c.at[mine], dst_ref=recv_c.at[mine], send_sem=crs_sem.at[0], recv_sem=crs_sem.at[1],
            device_id=me, device_id_type=LOGICAL,
        ).wait_recv()

    field_c = recv_c[...].reshape(128, LANES).T
    field_c = jnp.concatenate([field_c[:32], field_c[32:64]], axis=1)
    coarse_log = table_right(field_c, coarse_third)
    coarse_kappa = jnp.exp(coarse_log).reshape(PB // 2, QB // 2, N2 // 2)
    kc[pl.ds(2, PB // 2), pl.ds(EDGE, QB // 2)] = coarse_kappa
    ccol_s[0] = coarse_kappa[:, 0:2]
    ccol_s[1] = coarse_kappa[:, QB // 2 - 2 : QB // 2]
    for i, (dr, dc) in enumerate(DIRECTIONS[4:]):
        ccor_s[i, 0] = coarse_kappa[0 if dr < 0 else PB // 2 - 1, 0 if dc < 0 else QB // 2 - 1]
    for d in range(8):
        halo_start(d, "kappa", 1)

    def put_source(d, which):
        planes, width = (PB, QB) if which == 0 else (PB // 2, QB // 2)
        target, got = (fe, scol_r) if which == 0 else (fc, cscol_r)
        if d < 2:
            return None

        def store():
            at = EDGE - 1 if d == 2 else EDGE + width
            for plane in range(planes):
                target[1 + plane, pl.ds(at, 1)] = got[d - 2, plane]

        return store

    def put_kappa(d, which):
        planes, width = (PB, QB) if which == 0 else (PB // 2, QB // 2)
        target, cols, corners = (ke, col_r, cor_r) if which == 0 else (kc, ccol_r, ccor_r)
        if d < 2:
            return None

        def store():
            if d < 4:
                at = EDGE - 2 if d == 2 else EDGE + width
                for plane in range(planes):
                    target[2 + plane, pl.ds(at, 2)] = cols[d - 2, plane]
            else:
                dr, dc = DIRECTIONS[d]
                target[1 if dr < 0 else planes + 2, pl.ds(EDGE - 1 if dc < 0 else EDGE + width, 1)] = corners[d - 4]

        return store

    for d in range(4):
        for which in range(2):
            halo_wait(d, "source", which, put_source(d, which))
    for d in range(8):
        halo_wait(d, "kappa", 0, put_kappa(d, 0))
    smooth(ke, fe, ue, fine_out, PB, QB, N2)
    for d in range(8):
        halo_wait(d, "kappa", 1, put_kappa(d, 1))
    smooth(kc, fc, uc, coarse_out, PB // 2, QB // 2, N2 // 2)

    arrived.wait_send()
    back.wait_send()

    @pl.when(core == 0)
    def _():
        pltpu.make_async_remote_copy(
            src_ref=send_c.at[many], dst_ref=send_c.at[many], send_sem=crs_sem.at[0], recv_sem=crs_sem.at[1],
            device_id=me, device_id_type=LOGICAL,
        ).wait_send()


def body(noise, source):
    constants = tables()
    vmem, anywhere = pl.BlockSpec(memory_space=pltpu.VMEM), pl.BlockSpec(memory_space=pl.ANY)
    half_p, half_q, half_n = PB // 2, QB // 2, N2 // 2
    message = pltpu.VMEM((DEVICES, 2, LANES), F32)
    sems = pltpu.SemaphoreType.DMA
    return pl.pallas_call(
        kernel,
        out_shape=(
            jax.ShapeDtypeStruct((PB, QB, N2), F32),
            jax.ShapeDtypeStruct((half_p, half_q, half_n), F32),
        ),
        in_specs=[vmem, vmem] + [anywhere] * len(constants),
        out_specs=(vmem, vmem),
        scratch_shapes=[pltpu.VMEM(table.shape, table.dtype) for table in constants]
        + [message] * 4
        + [pltpu.VMEM((DEVICES, 1, LANES), F32), pltpu.VMEM((128, 1, LANES), F32)]
        + [
            pltpu.VMEM((PB + 4, QB + 16, N2), F32), pltpu.VMEM((PB + 2, QB + 16, N2), F32),
            pltpu.VMEM((PB + 2, QB + 16, N2), F32),
            pltpu.VMEM((half_p + 4, half_q + 16, half_n), F32), pltpu.VMEM((half_p + 2, half_q + 16, half_n), F32),
            pltpu.VMEM((half_p + 2, half_q + 16, half_n), F32),
        ]
        + [pltpu.VMEM((2, PB, 2, N2), F32)] * 2
        + [pltpu.VMEM((2, half_p, 2, half_n), F32)] * 2
        + [pltpu.VMEM((4, 1, N2), F32)] * 2
        + [pltpu.VMEM((4, 1, half_n), F32)] * 2
        + [pltpu.VMEM((2, PB, 1, N2), F32)] * 2
        + [pltpu.VMEM((2, half_p, 1, half_n), F32)] * 2
        + [sems((12,)), sems((2,)), sems((2,)), sems((2,)), sems]
        + [sems((8,))] * 4
        + [sems((4,))] * 4,
        compiler_params=pltpu.CompilerParams(collective_id=0, has_side_effects=True, vmem_limit_bytes=48 << 20),
    )(noise, source, *[jnp.asarray(table) for table in constants])


def solution(mesh):
    return jax.shard_map(
        body,
        mesh=mesh,
        in_specs=(P("row", ("level", "col"), None), P("row", ("level", "col"), None)),
        out_specs=(P("row", ("level", "col"), None), P("row", ("level", "col"), None)),
        check_vma=False,
    )
```

```python
import functools
import math

import jax
import jax.numpy as jnp
import ml_dtypes
import numpy as np
from jax import lax
from jax.experimental import pallas as pl
from jax.experimental.pallas import tpu as pltpu
from jax.sharding import PartitionSpec as P

JACOBI_WEIGHT = 2.0 / 3.0
CORRELATION = 0.2
FIELD_SCALE = 0.3
LOGICAL = pl.DeviceIdType.LOGICAL
F32 = jnp.float32
BF16 = jnp.bfloat16

N0, N1, N2 = 64, 512, 512
ROWS, COLS = 16, 16
DEVICES = ROWS * COLS
PB, QB = N0 // ROWS, N1 // COLS
LANES = PB * QB
EDGE = 8


def split_table(table):
    high = table.astype(ml_dtypes.bfloat16)
    low = (table - high.astype(np.float64)).astype(ml_dtypes.bfloat16)
    return high, low


def signed(index, length):
    return np.where(index < length // 2, index, index - length).astype(np.float64)


@functools.lru_cache(maxsize=None)
def tables():
    place = np.arange(DEVICES)
    r, c = place // COLS, place % COLS
    third = (r % 2) * 128 + (r // 2) * 16 + c
    turn = 2.0 * np.pi
    n2 = np.arange(N2)
    angle = turn * ((third[:, None] * n2[None, :]) % N2) / N2
    third_table = np.stack([np.cos(angle), -np.sin(angle)], axis=1).reshape(2 * DEVICES, N2)
    k2 = np.arange(128)
    angle = turn * ((k2[:, None] * np.arange(N2 // 2)[None, :]) % (N2 // 2)) / (N2 // 2)
    coarse_third = np.concatenate([np.cos(angle), -np.sin(angle)], axis=0)
    a, b = place // 16, place % 16
    angle = turn * ((a[:, None] * r[None, :] + b[:, None] * c[None, :]) % 16) / 16
    cos, sin = np.cos(angle), np.sin(angle)
    outer = np.concatenate([np.stack([cos, sin], axis=2), np.stack([-sin, cos], axis=2)], axis=0)
    outer = outer.reshape(2 * DEVICES, 2 * DEVICES)
    lane = np.arange(LANES)
    p, q = lane // QB, lane % QB
    angle = turn * (((8 * p[:, None] * p[None, :]) + q[:, None] * q[None, :]) % 32) / 32
    cos, sin = np.cos(angle), np.sin(angle)
    inner = np.block([[cos, -sin], [sin, cos]])
    lane_c = np.arange(32)
    pc, qc = lane_c // 16, lane_c % 16
    angle = turn * (((8 * p[:, None] * pc[None, :]) + q[:, None] * qc[None, :]) % 16) / 16
    cos, sin = np.cos(angle), np.sin(angle)
    empty = np.zeros((LANES, LANES - 64))
    inner_c = np.block([[cos, cos, empty, sin, sin, empty], [-sin, -sin, empty, cos, cos, empty]])
    angle = turn * ((8 * a[:, None] * p[None, :] + b[:, None] * q[None, :]) % 512) / 512
    twist = np.stack([np.cos(angle), np.sin(angle)])
    angle = turn * ((8 * a[:, None] * pc[None, :] + b[:, None] * qc[None, :]) % 256) / 256
    cos, sin = np.cos(angle), np.sin(angle)
    rest = np.zeros((DEVICES, LANES - 64))
    twist_c = np.stack([np.concatenate([cos, sin, rest], 1), np.concatenate([sin, -cos, rest], 1)])
    m0 = signed(a[:, None] + 16 * p[None, :], N0)
    m1 = signed(b[:, None] + 16 * q[None, :], N1)
    norm = (float(N0) * N1 * N2) ** -0.5
    inside = (m0 != -N0 // 2) & (m1 != -N1 // 2)
    inside_c = (np.abs(m0) < N0 // 4) & (np.abs(m1) < N1 // 4)
    waves = np.stack([m0 * m0 + m1 * m1, inside * FIELD_SCALE * norm, inside_c * FIELD_SCALE * norm])
    pool = (np.arange(N2)[:, None] // 2 == np.arange(N2 // 2)[None, :]).astype(ml_dtypes.bfloat16)
    pool_rows = (lane_c[:, None] == ((p // 2) * 16 + q // 2)[None, :]) * 0.125
    return (
        np.stack(split_table(third_table)),
        np.stack(split_table(outer)),
        np.stack(split_table(outer.T)),
        np.stack(split_table(inner)),
        np.stack(split_table(inner.T)),
        np.stack(split_table(inner_c)),
        np.stack(split_table(coarse_third)),
        pool,
        pool_rows.astype(ml_dtypes.bfloat16),
        twist.astype(np.float32),
        twist_c.astype(np.float32),
        waves.astype(np.float32),
    )


def halves(value):
    high = value.astype(BF16)
    return high, (value - high.astype(F32)).astype(BF16)


def dot(left, right):
    return jnp.dot(left, right, preferred_element_type=F32)


def table_left(table, value):
    high, low = halves(value)
    width = value.shape[1]
    both = dot(table[0], jnp.concatenate([high, low], axis=1))
    return both[:, :width] + (both[:, width:] + dot(table[1], high))


def table_right(value, table):
    high, low = halves(value)
    return dot(high, table[0]) + (dot(high, table[1]) + dot(low, table[0]))


DIRECTIONS = ((-1, 0), (1, 0), (0, -1), (0, 1), (-1, -1), (-1, 1), (1, -1), (1, 1))
OPPOSITE = (1, 0, 3, 2, 7, 6, 5, 4)


def flat_id(r, c):
    return (c // 8) * 128 + r * 8 + c % 8


def face_weight(center, beside):
    return jnp.where(beside > 0.0, 0.5 * (center + beside), center)


def smooth(kappa, source, first, out, planes, width, depth):
    tall = width + 2 * EDGE
    lane = lax.broadcasted_iota(jnp.int32, (tall, depth), 1)
    lane_in = lax.broadcasted_iota(jnp.int32, (width, depth), 1)
    diagonals = []
    for plane in range(planes + 2):
        center = kappa[plane + 1]
        diagonal = face_weight(center, kappa[plane + 2])
        diagonal = diagonal + face_weight(center, kappa[plane])
        diagonal = diagonal + face_weight(center, pltpu.roll(center, tall - 1, 0))
        diagonal = diagonal + face_weight(center, pltpu.roll(center, 1, 0))
        after = jnp.where(lane == depth - 1, 0.0, pltpu.roll(center, depth - 1, 1))
        before = jnp.where(lane == 0, 0.0, pltpu.roll(center, 1, 1))
        diagonal = diagonal + face_weight(center, after) + face_weight(center, before)
        guarded = jnp.where(center > 0.0, diagonal, 1.0)
        first[plane] = JACOBI_WEIGHT * source[plane] / guarded
    mid, low, high = pl.ds(EDGE, width), pl.ds(EDGE - 1, width), pl.ds(EDGE + 1, width)
    for plane in range(planes):
        center = kappa[plane + 2, mid]
        inner = first[plane + 1, mid]
        total = jnp.zeros_like(center)
        diagonal = jnp.zeros_like(center)
        for beside, value in (
            (kappa[plane + 3, mid], first[plane + 2, mid]),
            (kappa[plane + 1, mid], first[plane, mid]),
            (kappa[plane + 2, high], first[plane + 1, high]),
            (kappa[plane + 2, low], first[plane + 1, low]),
        ):
            face = face_weight(center, beside)
            diagonal = diagonal + face
            total = total + face * value
        for shift, missing in ((depth - 1, depth - 1), (1, 0)):
            outside = lane_in == missing
            beside = jnp.where(outside, 0.0, pltpu.roll(center, shift, 1))
            value = jnp.where(outside, 0.0, pltpu.roll(inner, shift, 1))
            face = face_weight(center, beside)
            diagonal = diagonal + face
            total = total + face * value
        residual = source[plane + 1, mid] - diagonal * inner + total
        out[plane] = inner + JACOBI_WEIGHT * residual / diagonal


def kernel(
    noise, source, third_h, outer_h, outer_t_h, inner_h, inner_t_h, inner_c_h, coarse_third_h, pool_h, pool_rows_h, twist_h, twist_c_h,
    waves_h, fine_out, coarse_out,
    third_t, outer, outer_t, inner, inner_t, inner_c, coarse_third, pool, pool_rows, twist, twist_c, waves,
    send_f, recv_f, send_i, recv_i, send_c, recv_c,
    ke, fe, ue, kc, fc, uc,
    col_s, col_r, ccol_s, ccol_r, cor_s, cor_r, ccor_s, ccor_r, scol_s, scol_r, cscol_s, cscol_r,
    table_sem, fwd_sem, inv_sem, crs_sem, own_sem, halo_s, halo_r, chalo_s, chalo_r, src_s, src_r, csrc_s, csrc_r,
):
    level, row, col = lax.axis_index("level"), lax.axis_index("row"), lax.axis_index("col")
    group = level * 8 + col
    me = flat_id(row, group)
    place = row * COLS + group
    core = row % 2

    for ref in (ke, fe, kc, fc):
        ref[...] = jnp.zeros_like(ref)

    barrier = pltpu.get_barrier_semaphore()

    columns = []
    for k in reversed(range(COLS)):
        y = lax.rem(col // 2 + k // 4, 4)
        x = lax.rem((col % 2) * 2 + level + k % 4, 4)
        x_hi, x_lo = x // 2, lax.rem(x, 2)
        columns.append((x_lo * 8 + y * 2 + x_hi, x_lo * 128 + y * 2 + x_hi))

    def row_at(i):
        j = i // 2
        half = (j + 1) // 2
        z = lax.rem(row // 2 + 4 + (1 - 2 * lax.rem(j, 2)) * half, 8)
        return z * 2 + lax.rem(core + 1 + i, 2)

    def for_all_peers(step):
        def one_row(i, carry):
            r = row_at(i)
            for c, part in columns:
                step(r * COLS + c, r * 8 + part)
            return carry

        lax.fori_loop(0, ROWS - 1, one_row, 0)
        for c, part in columns[:-1]:
            step(row * COLS + c, row * 8 + part)

    def greet(there, device):
        pl.semaphore_signal(barrier, inc=1, device_id=device, device_id_type=LOGICAL)

    for_all_peers(greet)

    pairs = (
        (third_h, third_t), (pool_h, pool), (pool_rows_h, pool_rows), (outer_h, outer), (twist_h, twist), (inner_h, inner), (waves_h, waves),
        (inner_t_h, inner_t), (inner_c_h, inner_c), (twist_c_h, twist_c), (outer_t_h, outer_t),
        (coarse_third_h, coarse_third),
    )
    loads = [pltpu.make_async_copy(a, b, table_sem.at[i]) for i, (a, b) in enumerate(pairs)]
    for load in loads:
        load.start()

    fe[pl.ds(1, PB), pl.ds(EDGE, QB)] = source[...].astype(F32)
    scol_s[0, :, 0] = source[:, 0].astype(F32)
    scol_s[1, :, 0] = source[:, QB - 1].astype(F32)
    loads[0].wait()
    noise_rows = noise[...].reshape(LANES, N2)
    contract = (((1,), (1,)), ((), ()))
    spectrum = lax.dot_general(third_t[0], noise_rows, contract, preferred_element_type=F32)
    spectrum = spectrum + lax.dot_general(third_t[1], noise_rows, contract, preferred_element_type=F32)
    send_f[...] = spectrum.reshape(DEVICES, 2, LANES)
    loads[1].wait()
    loads[2].wait()
    high, low = halves(dot(pool_rows[...], source[...].reshape(LANES, N2)))
    pooled = (dot(high, pool[...]) + dot(low, pool[...])).reshape(PB // 2, QB // 2, N2 // 2)
    fc[pl.ds(1, PB // 2), pl.ds(EDGE, QB // 2)] = pooled
    cscol_s[0, :, 0] = pooled[:, 0]
    cscol_s[1, :, 0] = pooled[:, QB // 2 - 1]

    pl.semaphore_wait(barrier, DEVICES - 1)

    def push(there, device):
        pltpu.make_async_remote_copy(
            src_ref=send_f.at[there], dst_ref=recv_f.at[place], send_sem=fwd_sem.at[0], recv_sem=fwd_sem.at[1],
            device_id=device, device_id_type=LOGICAL,
        ).start()

    for_all_peers(push)
    recv_f[place] = send_f[place]

    def neighbour(d):
        dr, dc = DIRECTIONS[d]
        r, c = row + dr, group + dc
        exists = (r >= 0) & (r < ROWS) & (c >= 0) & (c < COLS)
        return exists, flat_id(r, c)

    def halo_copies(d, kind):
        half_p, half_q = PB // 2, QB // 2
        mid, mid_c = pl.ds(EDGE, QB), pl.ds(EDGE, half_q)
        back = OPPOSITE[d]
        if kind == "source":
            if d < 2:
                here = (fe.at[1 if d == 0 else PB, mid], fe.at[PB + 1 if d == 0 else 0, mid], fe.at[0 if d == 0 else PB + 1, mid])
                there = (
                    fc.at[1 if d == 0 else half_p, mid_c], fc.at[half_p + 1 if d == 0 else 0, mid_c],
                    fc.at[0 if d == 0 else half_p + 1, mid_c],
                )
                return ((*here, src_s, src_r), (*there, csrc_s, csrc_r))
            return (
                (scol_s.at[d - 2], scol_r.at[back - 2], scol_r.at[d - 2], src_s, src_r),
                (cscol_s.at[d - 2], cscol_r.at[back - 2], cscol_r.at[d - 2], csrc_s, csrc_r),
            )
        if d < 2:
            return (
                (
                    ke.at[pl.ds(2 if d == 0 else PB, 2), mid], ke.at[pl.ds(PB + 2 if d == 0 else 0, 2), mid],
                    ke.at[pl.ds(0 if d == 0 else PB + 2, 2), mid], halo_s, halo_r,
                ),
                (
                    kc.at[pl.ds(2, 2), mid_c], kc.at[pl.ds(half_p + 2 if d == 0 else 0, 2), mid_c],
                    kc.at[pl.ds(0 if d == 0 else half_p + 2, 2), mid_c], chalo_s, chalo_r,
                ),
            )
        if d < 4:
            return (
                (col_s.at[d - 2], col_r.at[back - 2], col_r.at[d - 2], halo_s, halo_r),
                (ccol_s.at[d - 2], ccol_r.at[back - 2], ccol_r.at[d - 2], chalo_s, chalo_r),
            )
        return (
            (cor_s.at[d - 4], cor_r.at[back - 4], cor_r.at[d - 4], halo_s, halo_r),
            (ccor_s.at[d - 4], ccor_r.at[back - 4], ccor_r.at[d - 4], chalo_s, chalo_r),
        )

    def halo_start(d, kind, which):
        exists, there = neighbour(d)
        src, dst, _, s_sem, r_sem = halo_copies(d, kind)[which]

        @pl.when(exists)
        def _():
            pltpu.make_async_remote_copy(
                src_ref=src, dst_ref=dst, send_sem=s_sem.at[d], recv_sem=r_sem.at[OPPOSITE[d]], device_id=there,
                device_id_type=LOGICAL,
            ).start()

    def halo_wait(d, kind, which, then):
        exists, there = neighbour(d)
        src, _, here, s_sem, r_sem = halo_copies(d, kind)[which]

        @pl.when(exists)
        def _():
            copy = pltpu.make_async_remote_copy(
                src_ref=src, dst_ref=here, send_sem=s_sem.at[d], recv_sem=r_sem.at[d], device_id=there,
                device_id_type=LOGICAL,
            )
            copy.wait_send()
            copy.wait_recv()
            if then is not None:
                then()

    for d in range(4):
        for which in range(2):
            halo_start(d, "source", which)
    for load in loads[3:]:
        load.wait()

    many = pl.ds(0, DEVICES - 1)
    arrived = pltpu.make_async_remote_copy(
        src_ref=send_f.at[many], dst_ref=recv_f.at[many], send_sem=fwd_sem.at[0], recv_sem=fwd_sem.at[1], device_id=me,
        device_id_type=LOGICAL,
    )
    arrived.wait_recv()

    z = table_left(outer, recv_f[...].reshape(2 * DEVICES, LANES))
    z_re, z_im = z[:DEVICES], z[DEVICES:]
    turned = jnp.concatenate([z_re * twist[0] + z_im * twist[1], z_im * twist[0] - z_re * twist[1]], axis=1)
    y = table_right(turned, inner)
    third = core * 128 + (row // 2) * 16 + group
    third_f = third.astype(F32)
    weight = jnp.where(third == 0, 1.0, 2.0)
    damp = weight / (1.0 + (2.0 * math.pi * CORRELATION) ** 2 * (waves[0] + third_f * third_f))
    amp = waves[1] * damp
    amp_c = waves[2] * damp
    x = table_right(y * jnp.concatenate([amp, amp], axis=1), inner_t)
    x_re, x_im = x[:, :LANES], x[:, LANES:]
    xc = table_right(y * jnp.concatenate([amp_c, amp_c], axis=1), inner_c)
    xc_re, xc_im = xc[:, :LANES], xc[:, LANES:]
    fine_part = jnp.concatenate([x_re * twist[0] - x_im * twist[1], x_im * twist[0] + x_re * twist[1]], axis=0)
    coarse_part = jnp.concatenate(
        [xc_re * twist_c[0] - xc_im * twist_c[1], xc_im * twist_c[0] + xc_re * twist_c[1]], axis=0
    )
    both = jnp.concatenate([fine_part, coarse_part], axis=1)
    high, low = halves(both)
    planes = dot(outer_t[0], high) + (dot(outer_t[0], low) + dot(outer_t[1], high))
    send_i[...] = planes[:, :LANES].reshape(DEVICES, 2, LANES)
    send_c[...] = planes[:, LANES:].reshape(DEVICES, 2, LANES)[:, 0:1, :]

    def push_back(there, device):
        pltpu.make_async_remote_copy(
            src_ref=send_i.at[there], dst_ref=recv_i.at[place], send_sem=inv_sem.at[0], recv_sem=inv_sem.at[1],
            device_id=device, device_id_type=LOGICAL,
        ).start()

    coarse_place = (row // 2) * COLS + group

    def push_coarse(there, device):
        pltpu.make_async_remote_copy(
            src_ref=send_c.at[there], dst_ref=recv_c.at[coarse_place], send_sem=crs_sem.at[0],
            recv_sem=crs_sem.at[1], device_id=device, device_id_type=LOGICAL,
        ).start()

    for_all_peers(push_back)
    recv_i[place] = send_i[place]

    @pl.when(core == 0)
    def _():
        for_all_peers(push_coarse)
        recv_c[coarse_place] = send_c[place]

    back = pltpu.make_async_remote_copy(
        src_ref=send_i.at[many], dst_ref=recv_i.at[many], send_sem=inv_sem.at[0], recv_sem=inv_sem.at[1], device_id=me,
        device_id_type=LOGICAL,
    )
    back.wait_recv()
    field = recv_i[...].reshape(2 * DEVICES, LANES)
    fine_log = table_right(field.T, third_t)
    fine_kappa = jnp.exp(fine_log).reshape(PB, QB, N2)
    ke[pl.ds(2, PB), pl.ds(EDGE, QB)] = fine_kappa
    for d in range(2):
        halo_start(d, "kappa", 0)
    col_s[0] = fine_kappa[:, 0:2]
    col_s[1] = fine_kappa[:, QB - 2 : QB]
    for i, (dr, dc) in enumerate(DIRECTIONS[4:]):
        cor_s[i, 0] = fine_kappa[0 if dr < 0 else PB - 1, 0 if dc < 0 else QB - 1]
    for d in range(2, 8):
        halo_start(d, "kappa", 0)

    @pl.when(core == 0)
    def _():
        mine = pl.ds(0, 127)
        pltpu.make_async_remote_copy(
            src_ref=recv_c.at[mine], dst_ref=recv_c.at[mine], send_sem=crs_sem.at[0], recv_sem=crs_sem.at[1],
            device_id=me, device_id_type=LOGICAL,
        ).wait_recv()

    @pl.when(core == 1)
    def _():
        mine = pl.ds(0, 128)
        pltpu.make_async_remote_copy(
            src_ref=recv_c.at[mine], dst_ref=recv_c.at[mine], send_sem=crs_sem.at[0], recv_sem=crs_sem.at[1],
            device_id=me, device_id_type=LOGICAL,
        ).wait_recv()

    field_c = recv_c[...].reshape(128, LANES).T
    field_c = jnp.concatenate([field_c[:32], field_c[32:64]], axis=1)
    coarse_log = table_right(field_c, coarse_third)
    coarse_kappa = jnp.exp(coarse_log).reshape(PB // 2, QB // 2, N2 // 2)
    kc[pl.ds(2, PB // 2), pl.ds(EDGE, QB // 2)] = coarse_kappa
    ccol_s[0] = coarse_kappa[:, 0:2]
    ccol_s[1] = coarse_kappa[:, QB // 2 - 2 : QB // 2]
    for i, (dr, dc) in enumerate(DIRECTIONS[4:]):
        ccor_s[i, 0] = coarse_kappa[0 if dr < 0 else PB // 2 - 1, 0 if dc < 0 else QB // 2 - 1]
    for d in range(8):
        halo_start(d, "kappa", 1)

    def put_source(d, which):
        planes, width = (PB, QB) if which == 0 else (PB // 2, QB // 2)
        target, got = (fe, scol_r) if which == 0 else (fc, cscol_r)
        if d < 2:
            return None

        def store():
            at = EDGE - 1 if d == 2 else EDGE + width
            for plane in range(planes):
                target[1 + plane, pl.ds(at, 1)] = got[d - 2, plane]

        return store

    def put_kappa(d, which):
        planes, width = (PB, QB) if which == 0 else (PB // 2, QB // 2)
        target, cols, corners = (ke, col_r, cor_r) if which == 0 else (kc, ccol_r, ccor_r)
        if d < 2:
            return None

        def store():
            if d < 4:
                at = EDGE - 2 if d == 2 else EDGE + width
                for plane in range(planes):
                    target[2 + plane, pl.ds(at, 2)] = cols[d - 2, plane]
            else:
                dr, dc = DIRECTIONS[d]
                target[1 if dr < 0 else planes + 2, pl.ds(EDGE - 1 if dc < 0 else EDGE + width, 1)] = corners[d - 4]

        return store

    for d in range(4):
        for which in range(2):
            halo_wait(d, "source", which, put_source(d, which))
    for d in range(8):
        halo_wait(d, "kappa", 0, put_kappa(d, 0))
    smooth(ke, fe, ue, fine_out, PB, QB, N2)
    for d in range(8):
        halo_wait(d, "kappa", 1, put_kappa(d, 1))
    smooth(kc, fc, uc, coarse_out, PB // 2, QB // 2, N2 // 2)

    arrived.wait_send()
    back.wait_send()

    @pl.when(core == 0)
    def _():
        pltpu.make_async_remote_copy(
            src_ref=send_c.at[many], dst_ref=send_c.at[many], send_sem=crs_sem.at[0], recv_sem=crs_sem.at[1],
            device_id=me, device_id_type=LOGICAL,
        ).wait_send()


def body(noise, source):
    constants = tables()
    vmem, anywhere = pl.BlockSpec(memory_space=pltpu.VMEM), pl.BlockSpec(memory_space=pl.ANY)
    half_p, half_q, half_n = PB // 2, QB // 2, N2 // 2
    message = pltpu.VMEM((DEVICES, 2, LANES), F32)
    sems = pltpu.SemaphoreType.DMA
    return pl.pallas_call(
        kernel,
        out_shape=(
            jax.ShapeDtypeStruct((PB, QB, N2), F32),
            jax.ShapeDtypeStruct((half_p, half_q, half_n), F32),
        ),
        in_specs=[vmem, vmem] + [anywhere] * len(constants),
        out_specs=(vmem, vmem),
        scratch_shapes=[pltpu.VMEM(table.shape, table.dtype) for table in constants]
        + [message] * 4
        + [pltpu.VMEM((DEVICES, 1, LANES), F32), pltpu.VMEM((128, 1, LANES), F32)]
        + [
            pltpu.VMEM((PB + 4, QB + 16, N2), F32), pltpu.VMEM((PB + 2, QB + 16, N2), F32),
            pltpu.VMEM((PB + 2, QB + 16, N2), F32),
            pltpu.VMEM((half_p + 4, half_q + 16, half_n), F32), pltpu.VMEM((half_p + 2, half_q + 16, half_n), F32),
            pltpu.VMEM((half_p + 2, half_q + 16, half_n), F32),
        ]
        + [pltpu.VMEM((2, PB, 2, N2), F32)] * 2
        + [pltpu.VMEM((2, half_p, 2, half_n), F32)] * 2
        + [pltpu.VMEM((4, 1, N2), F32)] * 2
        + [pltpu.VMEM((4, 1, half_n), F32)] * 2
        + [pltpu.VMEM((2, PB, 1, N2), F32)] * 2
        + [pltpu.VMEM((2, half_p, 1, half_n), F32)] * 2
        + [sems((12,)), sems((2,)), sems((2,)), sems((2,)), sems]
        + [sems((8,))] * 4
        + [sems((4,))] * 4,
        compiler_params=pltpu.CompilerParams(collective_id=0, has_side_effects=True, vmem_limit_bytes=60 << 20),
    )(noise, source, *[jnp.asarray(table) for table in constants])


def solution(mesh):
    return jax.shard_map(
        body,
        mesh=mesh,
        in_specs=(P("row", ("level", "col"), None), P("row", ("level", "col"), None)),
        out_specs=(P("row", ("level", "col"), None), P("row", ("level", "col"), None)),
        check_vma=False,
    )
```

```python
import functools
import math

import jax
import jax.numpy as jnp
import ml_dtypes
import numpy as np
from jax import lax
from jax.experimental import pallas as pl
from jax.experimental.pallas import tpu as pltpu
from jax.sharding import PartitionSpec as P

JACOBI_WEIGHT = 2.0 / 3.0
CORRELATION = 0.2
FIELD_SCALE = 0.3
LOGICAL = pl.DeviceIdType.LOGICAL
F32 = jnp.float32
BF16 = jnp.bfloat16

N0, N1, N2 = 64, 512, 512
ROWS, COLS = 16, 16
DEVICES = ROWS * COLS
PB, QB = N0 // ROWS, N1 // COLS
LANES = PB * QB
CP, CQ = PB // 2 + 4, QB // 2 + 4
CELLS = CP * CQ
VMEM_LIMIT = 60 << 20
EDGE = 8


def split_table(table):
    high = table.astype(ml_dtypes.bfloat16)
    low = (table - high.astype(np.float64)).astype(ml_dtypes.bfloat16)
    return high, low


def signed(index, length):
    return np.where(index < length // 2, index, index - length).astype(np.float64)


def columns_of(column):
    y, x = column // 4, column % 4
    return (x % 2) * 8 + y * 2 + x // 2


@functools.lru_cache(maxsize=None)
def tables():
    place = np.arange(DEVICES)
    r, c = place % ROWS, columns_of(place // ROWS)
    third = (r % 2) * 128 + place // 2
    turn = 2.0 * np.pi
    n2 = np.arange(N2)
    angle = turn * ((third[:, None] * n2[None, :]) % N2) / N2
    third_table = np.stack([np.cos(angle), -np.sin(angle)], axis=1).reshape(2 * DEVICES, N2)
    k2 = np.arange(128)
    angle = turn * ((k2[:, None] * np.arange(N2 // 2)[None, :]) % (N2 // 2)) / (N2 // 2)
    coarse_third = np.stack([np.cos(angle), -np.sin(angle)], axis=1).reshape(256, N2 // 2)
    a, b = place // 16, place % 16
    angle = turn * ((a[:, None] * r[None, :] + b[:, None] * c[None, :]) % 16) / 16
    cos, sin = np.cos(angle), np.sin(angle)
    outer = np.concatenate([np.stack([cos, sin], axis=2), np.stack([-sin, cos], axis=2)], axis=0)
    outer = outer.reshape(2 * DEVICES, 2 * DEVICES)
    lane = np.arange(LANES)
    p, q = lane // QB, lane % QB
    angle = turn * (((8 * p[:, None] * p[None, :]) + q[:, None] * q[None, :]) % 32) / 32
    cos, sin = np.cos(angle), np.sin(angle)
    inner = np.block([[cos, -sin], [sin, cos]])
    lane_c = np.arange(CELLS)
    pc, qc = lane_c // CQ - 2, lane_c % CQ - 2
    angle = turn * (((8 * p[:, None] * pc[None, :]) + q[:, None] * qc[None, :]) % 16) / 16
    cos, sin = np.cos(angle), np.sin(angle)
    empty = np.zeros((LANES, LANES - CELLS))
    inner_c = np.block([[cos, empty, sin, empty], [-sin, empty, cos, empty]])
    angle = turn * ((8 * a[:, None] * p[None, :] + b[:, None] * q[None, :]) % 512) / 512
    twist = np.stack([np.cos(angle), np.sin(angle)])
    angle = turn * ((8 * a[:, None] * pc[None, :] + b[:, None] * qc[None, :]) % 256) / 256
    rest = np.zeros((DEVICES, LANES - CELLS))
    twist_c = np.stack([np.concatenate([np.cos(angle), rest], 1), np.concatenate([np.sin(angle), rest], 1)])
    m0 = signed(a[:, None] + 16 * p[None, :], N0)
    m1 = signed(b[:, None] + 16 * q[None, :], N1)
    norm = (float(N0) * N1 * N2) ** -0.5
    inside = (m0 != -N0 // 2) & (m1 != -N1 // 2)
    inside_c = (np.abs(m0) < N0 // 4) & (np.abs(m1) < N1 // 4)
    waves = np.stack([m0 * m0 + m1 * m1, inside * FIELD_SCALE * norm, inside_c * FIELD_SCALE * norm])
    pool = (np.arange(N2)[:, None] // 2 == np.arange(N2 // 2)[None, :]).astype(ml_dtypes.bfloat16)
    pool_rows = (np.arange(32)[:, None] == ((p // 2) * 16 + q // 2)[None, :]) * 0.125
    pool_rows = np.concatenate([pool_rows, np.zeros((32, LANES))], axis=1).astype(ml_dtypes.bfloat16)
    wide = np.concatenate([part for table in (third_table, outer, outer.T) for part in split_table(table)])
    narrow = np.concatenate([part for table in (inner, inner.T, inner_c, coarse_third) for part in split_table(table)])
    narrow = np.concatenate([narrow, pool, pool_rows])
    return wide, narrow, np.concatenate([twist, twist_c, waves]).astype(np.float32)


def halves(value):
    high = value.astype(BF16)
    return high, (value - high.astype(F32)).astype(BF16)


def dot(left, right):
    return jnp.dot(left, right, preferred_element_type=F32)


def table_left(table, value):
    high, low = halves(value)
    width = value.shape[1]
    both = dot(table[0], jnp.concatenate([high, low], axis=1))
    return both[:, :width] + (both[:, width:] + dot(table[1], high))


def table_right(value, table):
    high, low = halves(value)
    return dot(high, table[0]) + (dot(high, table[1]) + dot(low, table[0]))


DIRECTIONS = ((-1, 0), (1, 0), (0, -1), (0, 1), (-1, -1), (-1, 1), (1, -1), (1, 1))
OPPOSITE = (1, 0, 3, 2, 7, 6, 5, 4)


def flat_id(r, c):
    return (c // 8) * 128 + r * 8 + c % 8


def face_weight(center, beside):
    return jnp.where(beside > 0.0, 0.5 * (center + beside), center)


def smooth(kappa, source, first, out, planes, width, depth):
    tall = width + 2 * EDGE
    lane = lax.broadcasted_iota(jnp.int32, (tall, depth), 1)
    lane_in = lax.broadcasted_iota(jnp.int32, (width, depth), 1)
    diagonals = []
    for plane in range(planes + 2):
        center = kappa[plane + 1]
        diagonal = face_weight(center, kappa[plane + 2])
        diagonal = diagonal + face_weight(center, kappa[plane])
        diagonal = diagonal + face_weight(center, pltpu.roll(center, tall - 1, 0))
        diagonal = diagonal + face_weight(center, pltpu.roll(center, 1, 0))
        after = jnp.where(lane == depth - 1, 0.0, pltpu.roll(center, depth - 1, 1))
        before = jnp.where(lane == 0, 0.0, pltpu.roll(center, 1, 1))
        diagonal = diagonal + face_weight(center, after) + face_weight(center, before)
        guarded = jnp.where(center > 0.0, diagonal, 1.0)
        first[plane] = JACOBI_WEIGHT * source[plane] / guarded
    mid, low, high = pl.ds(EDGE, width), pl.ds(EDGE - 1, width), pl.ds(EDGE + 1, width)
    for plane in range(planes):
        center = kappa[plane + 2, mid]
        inner = first[plane + 1, mid]
        total = jnp.zeros_like(center)
        diagonal = jnp.zeros_like(center)
        for beside, value in (
            (kappa[plane + 3, mid], first[plane + 2, mid]),
            (kappa[plane + 1, mid], first[plane, mid]),
            (kappa[plane + 2, high], first[plane + 1, high]),
            (kappa[plane + 2, low], first[plane + 1, low]),
        ):
            face = face_weight(center, beside)
            diagonal = diagonal + face
            total = total + face * value
        for shift, missing in ((depth - 1, depth - 1), (1, 0)):
            outside = lane_in == missing
            beside = jnp.where(outside, 0.0, pltpu.roll(center, shift, 1))
            value = jnp.where(outside, 0.0, pltpu.roll(inner, shift, 1))
            face = face_weight(center, beside)
            diagonal = diagonal + face
            total = total + face * value
        residual = source[plane + 1, mid] - diagonal * inner + total
        out[plane] = inner + JACOBI_WEIGHT * residual / diagonal


def kernel(
    noise_h, source_h, wide_h, narrow_h, tables_h, fine_out, coarse_out,
    noise, source, wide, narrow, tables_v,
    send_f, recv_f, send_i, recv_i, send_c, recv_c,
    ke, fe, ue, kc, fc, uc,
    col_s, col_r, cor_s, cor_r, scol_s, scol_r, cscol_s, cscol_r,
    table_sem, fwd_sem, inv_sem, crs_sem, halo_s, halo_r, src_s, src_r, csrc_s, csrc_r,
):
    level, row, col = lax.axis_index("level"), lax.axis_index("row"), lax.axis_index("col")
    group = level * 8 + col
    me = flat_id(row, group)
    core, my_z = lax.rem(row, 2), row // 2
    my_y, my_x = col // 2, lax.rem(col, 2) * 2 + level
    place = (my_y * 4 + my_x) * ROWS + row
    half_p, half_q, half_n = PB // 2, QB // 2, N2 // 2

    rows = []
    for step in (4, 3, 5, 2, 6, 1, 7, 0):
        z2 = lax.rem(my_z + step, 8) * 2
        rows += [z2 + 1 - core, z2 + core]
    rows = [(r, r * 8) for r in rows]

    def far(i):
        return 2 + (1 - 2 * lax.rem(i, 2)) * ((i + 1) // 2)

    def for_column(i, j, step, count=ROWS):
        y, x = lax.rem(my_y + far(i), 4), lax.rem(my_x + far(j), 4)
        first, part = (y * 4 + x) * ROWS, lax.rem(x, 2) * 128 + y * 2 + x // 2
        for r, r8 in rows[:count]:
            step(first + r, part + r8)

    def for_all_peers(step):
        def one(i, carry):
            for_column(i // 4, lax.rem(i, 4), step)
            return carry

        lax.fori_loop(0, COLS - 1, one, 0)
        for_column(3, 3, step, ROWS - 1)

    barrier = pltpu.get_barrier_semaphore()

    def greet(there, device):
        pl.semaphore_signal(barrier, inc=1, device_id=device, device_id_type=LOGICAL)

    for ref in (ke, fe, fc):
        ref[...] = jnp.zeros_like(ref)

    for_all_peers(greet)

    size = 2 * DEVICES
    pairs = (
        (noise_h, noise), (source_h, source),
        (wide_h.at[pl.ds(0, 2 * size)], wide.at[pl.ds(0, 2 * size)]),
        (narrow_h, narrow), (tables_h, tables_v),
        (wide_h.at[pl.ds(2 * size, 4 * size)], wide.at[pl.ds(2 * size, 4 * size)]),
    )
    loads = [pltpu.make_async_copy(a, b, table_sem.at[i]) for i, (a, b) in enumerate(pairs)]
    for load in loads:
        load.start()

    class Parts:
        def __init__(self, ref, at, count):
            self.ref, self.at, self.count = ref, at, count

        def __getitem__(self, part):
            return self.ref[pl.ds(self.at + part * self.count, self.count)]

    third_t, outer, outer_t = (Parts(wide, i * 2 * size, size) for i in range(3))
    inner, inner_t, inner_c, coarse_third = (Parts(narrow, i * size, DEVICES) for i in range(4))
    twist, twist_c, waves = (tables_v.at[0], tables_v.at[1]), (tables_v.at[2], tables_v.at[3]), tables_v.at[pl.ds(4, 3)]

    loads[0].wait()
    loads[1].wait()
    loads[2].wait()
    noise_rows = noise[...].reshape(LANES, N2)
    contract = (((1,), (1,)), ((), ()))
    spectrum = lax.dot_general(third_t[0], noise_rows, contract, preferred_element_type=F32)
    spectrum = spectrum + lax.dot_general(third_t[1], noise_rows, contract, preferred_element_type=F32)
    send_f[...] = spectrum.reshape(DEVICES, 2, LANES)

    fe[pl.ds(1, PB), pl.ds(EDGE, QB)] = source[...].astype(F32)
    scol_s[0, :, 0] = source[:, 0].astype(F32)
    scol_s[1, :, 0] = source[:, QB - 1].astype(F32)

    pl.semaphore_wait(barrier, DEVICES - 1)

    def push(there, device):
        pltpu.make_async_remote_copy(
            src_ref=send_f.at[there], dst_ref=recv_f.at[place], send_sem=fwd_sem.at[0], recv_sem=fwd_sem.at[1],
            device_id=device, device_id_type=LOGICAL,
        ).start()

    for_all_peers(push)
    recv_f[place] = send_f[place]

    loads[3].wait()
    loads[4].wait()
    high, low = halves(dot(narrow[pl.ds(5 * size, 32), pl.ds(0, LANES)], source[...].reshape(LANES, N2)))
    pool = narrow[pl.ds(4 * size, size)]
    pooled = (dot(high, pool) + dot(low, pool)).reshape(half_p, half_q, half_n)
    fc[pl.ds(1, half_p), pl.ds(EDGE, half_q)] = pooled
    cscol_s[0, :, 0] = pooled[:, 0]
    cscol_s[1, :, 0] = pooled[:, half_q - 1]

    def neighbour(d):
        dr, dc = DIRECTIONS[d]
        r, c = row + dr, group + dc
        exists = (r >= 0) & (r < ROWS) & (c >= 0) & (c < COLS)
        return exists, flat_id(r, c)

    mid, mid_c = pl.ds(EDGE, QB), pl.ds(EDGE, half_q)

    def halo_copy(d, kind):
        back = OPPOSITE[d]
        if kind == "source":
            if d < 2:
                return (
                    fe.at[1 if d == 0 else PB, mid], fe.at[PB + 1 if d == 0 else 0, mid],
                    fe.at[0 if d == 0 else PB + 1, mid], src_s, src_r,
                )
            return scol_s.at[d - 2], scol_r.at[back - 2], scol_r.at[d - 2], src_s, src_r
        if kind == "coarse":
            if d < 2:
                return (
                    fc.at[1 if d == 0 else half_p, mid_c], fc.at[half_p + 1 if d == 0 else 0, mid_c],
                    fc.at[0 if d == 0 else half_p + 1, mid_c], csrc_s, csrc_r,
                )
            return cscol_s.at[d - 2], cscol_r.at[back - 2], cscol_r.at[d - 2], csrc_s, csrc_r
        if d < 2:
            return (
                ke.at[pl.ds(2 if d == 0 else PB, 2), mid], ke.at[pl.ds(PB + 2 if d == 0 else 0, 2), mid],
                ke.at[pl.ds(0 if d == 0 else PB + 2, 2), mid], halo_s, halo_r,
            )
        if d < 4:
            return col_s.at[d - 2], col_r.at[back - 2], col_r.at[d - 2], halo_s, halo_r
        return cor_s.at[d - 4], cor_r.at[back - 4], cor_r.at[d - 4], halo_s, halo_r

    def halo_start(d, kind):
        exists, there = neighbour(d)
        src, dst, _, s_sem, r_sem = halo_copy(d, kind)

        @pl.when(exists)
        def _():
            pltpu.make_async_remote_copy(
                src_ref=src, dst_ref=dst, send_sem=s_sem.at[d], recv_sem=r_sem.at[OPPOSITE[d]], device_id=there,
                device_id_type=LOGICAL,
            ).start()

    def halo_wait(d, kind, then):
        exists, there = neighbour(d)
        src, _, here, s_sem, r_sem = halo_copy(d, kind)

        @pl.when(exists)
        def _():
            copy = pltpu.make_async_remote_copy(
                src_ref=src, dst_ref=here, send_sem=s_sem.at[d], recv_sem=r_sem.at[d], device_id=there,
                device_id_type=LOGICAL,
            )
            copy.wait_send()
            copy.wait_recv()
            then(d)

    for d in range(4):
        halo_start(d, "source")
        halo_start(d, "coarse")

    third = core * 128 + place // 2
    third_f = third.astype(F32)
    weight = jnp.where(third == 0, 1.0, 2.0)
    damp = weight / (1.0 + (2.0 * math.pi * CORRELATION) ** 2 * (waves[0] + third_f * third_f))
    amp = waves[1] * damp
    amp_c = waves[2] * damp
    loads[5].wait()

    many = pl.ds(0, DEVICES - 1)
    arrived = pltpu.make_async_remote_copy(
        src_ref=send_f.at[many], dst_ref=recv_f.at[many], send_sem=fwd_sem.at[0], recv_sem=fwd_sem.at[1], device_id=me,
        device_id_type=LOGICAL,
    )
    arrived.wait_recv()

    z = table_left(outer, recv_f[...].reshape(size, LANES))
    z_re, z_im = z[:DEVICES], z[DEVICES:]
    cos, sin = twist[0][...], twist[1][...]
    turned = jnp.concatenate([z_re * cos + z_im * sin, z_im * cos - z_re * sin], axis=1)
    y = table_right(turned, inner)
    x = table_right(y * jnp.concatenate([amp, amp], axis=1), inner_t)
    x_re, x_im = x[:, :LANES], x[:, LANES:]
    xc = table_right(y * jnp.concatenate([amp_c, amp_c], axis=1), inner_c)
    xc_re, xc_im = xc[:, :LANES], xc[:, LANES:]
    cos_c, sin_c = twist_c[0][...], twist_c[1][...]
    fine_part = jnp.concatenate([x_re * cos - x_im * sin, x_im * cos + x_re * sin], axis=0)
    coarse_part = jnp.concatenate([xc_re * cos_c - xc_im * sin_c, xc_im * cos_c + xc_re * sin_c], axis=0)
    high, low = halves(jnp.concatenate([fine_part, coarse_part], axis=1))

    def push_back(there, device):
        pltpu.make_async_remote_copy(
            src_ref=send_i.at[there], dst_ref=recv_i.at[place], send_sem=inv_sem.at[0], recv_sem=inv_sem.at[1],
            device_id=device, device_id_type=LOGICAL,
        ).start()

    coarse_place = place // 2

    def push_coarse(there, device):
        pltpu.make_async_remote_copy(
            src_ref=send_c.at[there], dst_ref=recv_c.at[coarse_place], send_sem=crs_sem.at[0],
            recv_sem=crs_sem.at[1], device_id=device, device_id_type=LOGICAL,
        ).start()

    for i in range(4):
        y4 = lax.rem(my_y + (2, 1, 3, 0)[i], 4)
        upper = wide[pl.ds(4 * size + y4 * LANES, LANES)]
        lower = wide[pl.ds(5 * size + y4 * LANES, LANES)]
        planes = dot(upper, high) + (dot(upper, low) + dot(lower, high))
        send_i[pl.ds(y4 * 64, 64)] = planes[:, :LANES].reshape(64, 2, LANES)
        send_c[pl.ds(y4 * 64, 64)] = planes[:, LANES:].reshape(64, 2, LANES)

        def one(j, carry, i=i):
            for_column(i, j, push_back)
            return carry

        if i < 3:
            lax.fori_loop(0, 4, one, 0)
        else:
            lax.fori_loop(0, 3, one, 0)
            for_column(3, 3, push_back, ROWS - 1)
    recv_i[place] = send_i[place]

    @pl.when(core == 0)
    def _():
        for_all_peers(push_coarse)
        recv_c[coarse_place] = send_c[place]

    def put_source(d):
        if d >= 2:
            at = EDGE - 1 if d == 2 else EDGE + QB
            for plane in range(PB):
                fe[1 + plane, pl.ds(at, 1)] = scol_r[d - 2, plane]

    def put_coarse(d):
        if d >= 2:
            at = EDGE - 1 if d == 2 else EDGE + half_q
            for plane in range(half_p):
                fc[1 + plane, pl.ds(at, 1)] = cscol_r[d - 2, plane]

    def put_kappa(d):
        dr, dc = DIRECTIONS[d]
        if d >= 4:
            ke[1 if dr < 0 else PB + 2, pl.ds(EDGE - 1 if dc < 0 else EDGE + QB, 1)] = cor_r[d - 4]
        elif d >= 2:
            at = EDGE - 2 if d == 2 else EDGE + QB
            for plane in range(PB):
                ke[2 + plane, pl.ds(at, 2)] = col_r[d - 2, plane]

    for d in range(4):
        halo_wait(d, "source", put_source)
        halo_wait(d, "coarse", put_coarse)
    kc[...] = jnp.zeros_like(kc)
    arrived.wait_send()

    returned = pltpu.make_async_remote_copy(
        src_ref=send_i.at[many], dst_ref=recv_i.at[many], send_sem=inv_sem.at[0], recv_sem=inv_sem.at[1], device_id=me,
        device_id_type=LOGICAL,
    )
    returned.wait_recv()
    fine_log = table_right(recv_i[...].reshape(size, LANES).T, third_t)
    fine_kappa = jnp.exp(fine_log).reshape(PB, QB, N2)
    for i, (dr, dc) in enumerate(DIRECTIONS[4:]):
        cor_s[i, 0] = fine_kappa[0 if dr < 0 else PB - 1, 0 if dc < 0 else QB - 1]
    col_s[0] = fine_kappa[:, 0:2]
    col_s[1] = fine_kappa[:, QB - 2 : QB]
    ke[pl.ds(2, PB), mid] = fine_kappa
    for d in (4, 5, 6, 7, 2, 3, 0, 1):
        halo_start(d, "kappa")

    for own in range(2):

        @pl.when(core == own)
        def _(own=own):
            some = pl.ds(0, 127 + own)
            pltpu.make_async_remote_copy(
                src_ref=recv_c.at[some], dst_ref=recv_c.at[some], send_sem=crs_sem.at[0], recv_sem=crs_sem.at[1],
                device_id=me, device_id_type=LOGICAL,
            ).wait_recv()

    coarse_log = table_right(recv_c[...].reshape(DEVICES, LANES).T, coarse_third)
    cell = lax.broadcasted_iota(jnp.int32, (LANES, half_n), 0)
    n0 = row * half_p + lax.div(cell, CQ) - 2
    n1 = group * half_q + lax.rem(cell, CQ) - 2
    inside = (n0 >= 0) & (n0 < N0 // 2) & (n1 >= 0) & (n1 < N1 // 2)
    coarse_kappa = jnp.where(inside, jnp.exp(coarse_log), 0.0)
    for plane in range(CP):
        kc[plane, pl.ds(EDGE - 2, CQ)] = coarse_kappa[plane * CQ : (plane + 1) * CQ]
    smooth(kc, fc, uc, coarse_out, half_p, half_q, half_n)

    for d in (0, 1, 2, 3, 4, 5, 6, 7):
        halo_wait(d, "kappa", put_kappa)
    smooth(ke, fe, ue, fine_out, PB, QB, N2)

    returned.wait_send()

    @pl.when(core == 0)
    def _():
        pltpu.make_async_remote_copy(
            src_ref=send_c.at[many], dst_ref=send_c.at[many], send_sem=crs_sem.at[0], recv_sem=crs_sem.at[1],
            device_id=me, device_id_type=LOGICAL,
        ).wait_send()


def hand_over(fine, coarse, fine_out, coarse_out):
    fine_out[...] = fine[...]
    coarse_out[...] = coarse[...]


def body(noise, source):
    constants = tables()
    vmem, anywhere = pl.BlockSpec(memory_space=pltpu.VMEM), pl.BlockSpec(memory_space=pl.ANY)
    half_p, half_q, half_n = PB // 2, QB // 2, N2 // 2
    message = pltpu.VMEM((DEVICES, 2, LANES), F32)
    sems = pltpu.SemaphoreType.DMA
    pressures = pl.pallas_call(
        kernel,
        out_shape=(
            jax.ShapeDtypeStruct((PB, QB, N2), F32),
            jax.ShapeDtypeStruct((half_p, half_q, half_n), F32),
        ),
        in_specs=[anywhere] * 5,
        out_specs=(vmem, vmem),
        scratch_shapes=[pltpu.VMEM((PB, QB, N2), BF16)] * 2
        + [pltpu.VMEM(table.shape, table.dtype) for table in constants]
        + [message] * 5
        + [pltpu.VMEM((128, 2, LANES), F32)]
        + [
            pltpu.VMEM((PB + 4, QB + 16, N2), F32), pltpu.VMEM((PB + 2, QB + 16, N2), F32),
            pltpu.VMEM((PB + 2, QB + 16, N2), F32),
            pltpu.VMEM((half_p + 4, half_q + 16, half_n), F32), pltpu.VMEM((half_p + 2, half_q + 16, half_n), F32),
            pltpu.VMEM((half_p + 2, half_q + 16, half_n), F32),
        ]
        + [pltpu.VMEM((2, PB, 2, N2), F32)] * 2
        + [pltpu.VMEM((4, 1, N2), F32)] * 2
        + [pltpu.VMEM((2, PB, 1, N2), F32)] * 2
        + [pltpu.VMEM((2, half_p, 1, half_n), F32)] * 2
        + [sems((6,)), sems((2,)), sems((2,)), sems((2,))]
        + [sems((8,))] * 2
        + [sems((4,))] * 4,
        compiler_params=pltpu.CompilerParams(collective_id=0, has_side_effects=True, vmem_limit_bytes=VMEM_LIMIT),
    )(noise, source, *[jnp.asarray(table) for table in constants])
    return pl.pallas_call(
        hand_over,
        out_shape=tuple(jax.ShapeDtypeStruct(value.shape, value.dtype) for value in pressures),
        in_specs=[vmem] * 2,
        out_specs=(vmem, vmem),
    )(*pressures)


def solution(mesh):
    return jax.shard_map(
        body,
        mesh=mesh,
        in_specs=(P("row", ("level", "col"), None), P("row", ("level", "col"), None)),
        out_specs=(P("row", ("level", "col"), None), P("row", ("level", "col"), None)),
        check_vma=False,
    )
```

```python
import functools
import math

import jax
import jax.numpy as jnp
import ml_dtypes
import numpy as np
from jax import lax
from jax.experimental import pallas as pl
from jax.experimental.pallas import tpu as pltpu
from jax.sharding import PartitionSpec as P

JACOBI_WEIGHT = 2.0 / 3.0
CORRELATION = 0.2
FIELD_SCALE = 0.3
LOGICAL = pl.DeviceIdType.LOGICAL
F32 = jnp.float32
BF16 = jnp.bfloat16

N0, N1, N2 = 64, 512, 512
ROWS, COLS = 16, 16
DEVICES = ROWS * COLS
PB, QB = N0 // ROWS, N1 // COLS
LANES = PB * QB
CP, CQ = PB // 2 + 4, QB // 2 + 4
CELLS = CP * CQ
VMEM_LIMIT = 60 << 20
FAR = (2, 1, 3, 0)
EDGE = 8


def split_table(table):
    high = table.astype(ml_dtypes.bfloat16)
    low = (table - high.astype(np.float64)).astype(ml_dtypes.bfloat16)
    return high, low


def signed(index, length):
    return np.where(index < length // 2, index, index - length).astype(np.float64)


def columns_of(column):
    y, x = column // 4, column % 4
    return (x % 2) * 8 + y * 2 + x // 2


@functools.lru_cache(maxsize=None)
def tables():
    place = np.arange(DEVICES)
    r, c = place % ROWS, columns_of(place // ROWS)
    third = (r % 2) * 128 + place // 2
    turn = 2.0 * np.pi
    n2 = np.arange(N2)
    angle = turn * ((third[:, None] * n2[None, :]) % N2) / N2
    third_table = np.stack([np.cos(angle), -np.sin(angle)], axis=1).reshape(2 * DEVICES, N2)
    k2 = np.arange(128)
    angle = turn * ((k2[:, None] * np.arange(N2 // 2)[None, :]) % (N2 // 2)) / (N2 // 2)
    coarse_third = np.stack([np.cos(angle), -np.sin(angle)], axis=1).reshape(256, N2 // 2)
    a, b = place // 16, place % 16
    angle = turn * ((a[:, None] * r[None, :] + b[:, None] * c[None, :]) % 16) / 16
    cos, sin = np.cos(angle), np.sin(angle)
    outer = np.concatenate([np.stack([cos, sin], axis=2), np.stack([-sin, cos], axis=2)], axis=0)
    outer = outer.reshape(2 * DEVICES, 2 * DEVICES)
    lane = np.arange(LANES)
    p, q = lane // QB, lane % QB
    angle = turn * (((8 * p[:, None] * p[None, :]) + q[:, None] * q[None, :]) % 32) / 32
    cos, sin = np.cos(angle), np.sin(angle)
    inner = np.block([[cos, -sin], [sin, cos]])
    lane_c = np.arange(CELLS)
    pc, qc = lane_c // CQ - 2, lane_c % CQ - 2
    angle = turn * (((8 * p[:, None] * pc[None, :]) + q[:, None] * qc[None, :]) % 16) / 16
    cos, sin = np.cos(angle), np.sin(angle)
    empty = np.zeros((LANES, LANES - CELLS))
    inner_c = np.block([[cos, empty, sin, empty], [-sin, empty, cos, empty]])
    angle = turn * ((8 * a[:, None] * p[None, :] + b[:, None] * q[None, :]) % 512) / 512
    twist = np.stack([np.cos(angle), np.sin(angle)])
    angle = turn * ((8 * a[:, None] * pc[None, :] + b[:, None] * qc[None, :]) % 256) / 256
    rest = np.zeros((DEVICES, LANES - CELLS))
    twist_c = np.stack([np.concatenate([np.cos(angle), rest], 1), np.concatenate([np.sin(angle), rest], 1)])
    m0 = signed(a[:, None] + 16 * p[None, :], N0)
    m1 = signed(b[:, None] + 16 * q[None, :], N1)
    norm = (float(N0) * N1 * N2) ** -0.5
    inside = (m0 != -N0 // 2) & (m1 != -N1 // 2)
    inside_c = (np.abs(m0) < N0 // 4) & (np.abs(m1) < N1 // 4)
    waves = np.stack([m0 * m0 + m1 * m1, inside * FIELD_SCALE * norm, inside_c * FIELD_SCALE * norm])
    pool = (np.arange(N2)[:, None] // 2 == np.arange(N2 // 2)[None, :]).astype(ml_dtypes.bfloat16)
    pool_rows = (np.arange(32)[:, None] == ((p // 2) * 16 + q // 2)[None, :]) * 0.125
    pool_rows = np.concatenate([pool_rows, np.zeros((32, LANES))], axis=1).astype(ml_dtypes.bfloat16)
    wide = np.concatenate([part for table in (third_table, outer, outer.T) for part in split_table(table)])
    narrow = np.concatenate([part for table in (inner, inner.T, inner_c, coarse_third) for part in split_table(table)])
    narrow = np.concatenate([narrow, pool, pool_rows])
    return wide, narrow, np.concatenate([twist, twist_c, waves]).astype(np.float32)


def halves(value):
    high = value.astype(BF16)
    return high, (value - high.astype(F32)).astype(BF16)


def dot(left, right):
    return jnp.dot(left, right, preferred_element_type=F32)


def table_right(value, table):
    high, low = halves(value)
    return dot(high, table[0]) + (dot(high, table[1]) + dot(low, table[0]))


DIRECTIONS = ((-1, 0), (1, 0), (0, -1), (0, 1), (-1, -1), (-1, 1), (1, -1), (1, 1))
OPPOSITE = (1, 0, 3, 2, 7, 6, 5, 4)


def flat_id(r, c):
    return (c // 8) * 128 + r * 8 + c % 8


def face_weight(center, beside):
    return jnp.where(beside > 0.0, 0.5 * (center + beside), center)


def beside_lanes(value, missing):
    depth = value.shape[-1]
    lane = lax.broadcasted_iota(jnp.int32, value.shape, 1)
    after = jnp.where(lane == depth - 1, missing, pltpu.roll(value, depth - 1, 1))
    before = jnp.where(lane == 0, missing, pltpu.roll(value, 1, 1))
    return after, before


def first_sweep(center, neighbours, source):
    diagonal = face_weight(center, neighbours[0])
    for beside in neighbours[1:]:
        diagonal = diagonal + face_weight(center, beside)
    return JACOBI_WEIGHT * source / jnp.where(center > 0.0, diagonal, 1.0)


def smooth(kappa, source, first, out, planes, width):
    mid, low, high = pl.ds(EDGE, width), pl.ds(EDGE - 1, width), pl.ds(EDGE + 1, width)
    for plane in range(planes + 2):
        center = kappa[plane + 1, mid]
        near = (kappa[plane + 2, mid], kappa[plane, mid], kappa[plane + 1, high], kappa[plane + 1, low])
        first[plane, mid] = first_sweep(center, near + beside_lanes(center, 0.0), source[plane, mid])
    for at, inward, outward in ((EDGE - 1, EDGE, EDGE - 2), (EDGE + width, EDGE + width - 1, EDGE + width + 1)):

        def line(ref, base, q):
            return jnp.concatenate([ref[base + plane, pl.ds(q, 1)] for plane in range(planes)], axis=0)

        center = line(kappa, 2, at)
        near = (line(kappa, 3, at), line(kappa, 1, at), line(kappa, 2, inward), line(kappa, 2, outward))
        value = first_sweep(center, near + beside_lanes(center, 0.0), line(source, 1, at))
        for plane in range(planes):
            first[1 + plane, pl.ds(at, 1)] = value[plane : plane + 1]
    for plane in range(planes):
        center = kappa[plane + 2, mid]
        inner = first[plane + 1, mid]
        total = jnp.zeros_like(center)
        diagonal = jnp.zeros_like(center)
        after, before = beside_lanes(center, 0.0)
        after_value, before_value = beside_lanes(inner, 0.0)
        for beside, value in (
            (kappa[plane + 3, mid], first[plane + 2, mid]),
            (kappa[plane + 1, mid], first[plane, mid]),
            (kappa[plane + 2, high], first[plane + 1, high]),
            (kappa[plane + 2, low], first[plane + 1, low]),
            (after, after_value),
            (before, before_value),
        ):
            face = face_weight(center, beside)
            diagonal = diagonal + face
            total = total + face * value
        residual = source[plane + 1, mid] - diagonal * inner + total
        out[plane] = inner + JACOBI_WEIGHT * residual / diagonal


def kernel(
    noise_h, source_h, wide_h, narrow_h, tables_h, fine_out, coarse_out,
    noise, source, wide, narrow, tables_v,
    send_f, recv_f, send_i, recv_i, send_c, recv_c,
    ke, fe, ue, kc, fc, uc,
    col_s, col_r, cor_s, cor_r, scol_s, scol_r, cscol_s, cscol_r,
    table_sem, fwd_s, fwd_r, inv_s, inv_r, crs_sem, halo_s, halo_r, src_s, src_r, csrc_s, csrc_r,
):
    level, row, col = lax.axis_index("level"), lax.axis_index("row"), lax.axis_index("col")
    group = level * 8 + col
    me = flat_id(row, group)
    core, my_z = lax.rem(row, 2), row // 2
    my_y, my_x = col // 2, lax.rem(col, 2) * 2 + level
    place = (my_y * 4 + my_x) * ROWS + row
    half_p, half_q, half_n = PB // 2, QB // 2, N2 // 2

    rows = []
    for step in (4, 3, 5, 2, 6, 1, 7, 0):
        z2 = lax.rem(my_z + step, 8) * 2
        rows += [z2 + 1 - core, z2 + core]
    rows = [(r, r * 8) for r in rows]

    def far(j):
        return 2 + (1 - 2 * lax.rem(j, 2)) * ((j + 1) // 2)

    def for_column(i, j, step, count=ROWS):
        y, x = lax.rem(my_y + FAR[i], 4), lax.rem(my_x + far(j), 4)
        first, part = (y * 4 + x) * ROWS, lax.rem(x, 2) * 128 + y * 2 + x // 2
        for r, r8 in rows[:count]:
            step(i, first + r, part + r8)

    def for_quarter(i, step):
        def one(j, carry):
            for_column(i, j, step)
            return carry

        if i < 3:
            lax.fori_loop(0, 4, one, 0)
        else:
            lax.fori_loop(0, 3, one, 0)
            for_column(3, 3, step, ROWS - 1)

    def for_all_peers(step):
        for i in range(4):
            for_quarter(i, step)

    barrier = pltpu.get_barrier_semaphore()

    def greet(i, there, device):
        pl.semaphore_signal(barrier, inc=1, device_id=device, device_id_type=LOGICAL)

    for_all_peers(greet)

    size = 2 * DEVICES
    pairs = (
        (noise_h, noise), (source_h, source),
        (wide_h.at[pl.ds(0, 2 * size)], wide.at[pl.ds(0, 2 * size)]),
        (narrow_h, narrow), (tables_h, tables_v),
        (wide_h.at[pl.ds(2 * size, 4 * size)], wide.at[pl.ds(2 * size, 4 * size)]),
    )
    loads = [pltpu.make_async_copy(a, b, table_sem.at[i]) for i, (a, b) in enumerate(pairs)]
    for load in loads:
        load.start()

    class Parts:
        def __init__(self, ref, at, count):
            self.ref, self.at, self.count = ref, at, count

        def __getitem__(self, part):
            return self.ref[pl.ds(self.at + part * self.count, self.count)]

    third_t = Parts(wide, 0, size)
    inner, inner_t, inner_c, coarse_third = (Parts(narrow, i * size, DEVICES) for i in range(4))
    twist, twist_c, waves = (tables_v.at[0], tables_v.at[1]), (tables_v.at[2], tables_v.at[3]), tables_v.at[pl.ds(4, 3)]

    for ref, width in ((ke, QB), (fe, QB), (fc, half_q)):
        for at in (0, EDGE + width):
            ref[:, pl.ds(at, EDGE)] = jnp.zeros((ref.shape[0], EDGE, ref.shape[2]), F32)

    for edge, last in ((0, False), (ROWS - 1, True)):

        @pl.when(row == edge)
        def _(last=last):
            for ref, width, layers in ((ke, QB, 2), (fe, QB, 1), (fc, half_q, 1)):
                at = ref.shape[0] - layers if last else 0
                ref[pl.ds(at, layers), pl.ds(EDGE, width)] = jnp.zeros((layers, width, ref.shape[2]), F32)

    loads[0].wait()
    loads[1].wait()
    loads[2].wait()
    noise_rows = noise[...].reshape(LANES, N2)
    contract = (((1,), (1,)), ((), ()))
    spectrum = lax.dot_general(third_t[0], noise_rows, contract, preferred_element_type=F32)
    spectrum = spectrum + lax.dot_general(third_t[1], noise_rows, contract, preferred_element_type=F32)
    send_f[...] = spectrum.reshape(DEVICES, 2, LANES)

    fe[pl.ds(1, PB), pl.ds(EDGE, QB)] = source[...].astype(F32)
    scol_s[0, :, 0] = source[:, 0].astype(F32)
    scol_s[1, :, 0] = source[:, QB - 1].astype(F32)

    pl.semaphore_wait(barrier, DEVICES - 1)

    def push(i, there, device):
        pltpu.make_async_remote_copy(
            src_ref=send_f.at[there], dst_ref=recv_f.at[place], send_sem=fwd_s, recv_sem=fwd_r.at[i],
            device_id=device, device_id_type=LOGICAL,
        ).start()

    for_all_peers(push)
    recv_f[place] = send_f[place]

    loads[3].wait()
    loads[4].wait()
    high, low = halves(dot(narrow[pl.ds(5 * size, 32), pl.ds(0, LANES)], source[...].reshape(LANES, N2)))
    pool = narrow[pl.ds(4 * size, size)]
    pooled = (dot(high, pool) + dot(low, pool)).reshape(half_p, half_q, half_n)
    fc[pl.ds(1, half_p), pl.ds(EDGE, half_q)] = pooled
    cscol_s[0, :, 0] = pooled[:, 0]
    cscol_s[1, :, 0] = pooled[:, half_q - 1]

    def neighbour(d):
        dr, dc = DIRECTIONS[d]
        r, c = row + dr, group + dc
        exists = (r >= 0) & (r < ROWS) & (c >= 0) & (c < COLS)
        return exists, flat_id(r, c)

    mid, mid_c = pl.ds(EDGE, QB), pl.ds(EDGE, half_q)

    def halo_copy(d, kind):
        back = OPPOSITE[d]
        if kind == "source":
            if d < 2:
                return (
                    fe.at[1 if d == 0 else PB, mid], fe.at[PB + 1 if d == 0 else 0, mid],
                    fe.at[0 if d == 0 else PB + 1, mid], src_s, src_r,
                )
            return scol_s.at[d - 2], scol_r.at[back - 2], scol_r.at[d - 2], src_s, src_r
        if kind == "coarse":
            if d < 2:
                return (
                    fc.at[1 if d == 0 else half_p, mid_c], fc.at[half_p + 1 if d == 0 else 0, mid_c],
                    fc.at[0 if d == 0 else half_p + 1, mid_c], csrc_s, csrc_r,
                )
            return cscol_s.at[d - 2], cscol_r.at[back - 2], cscol_r.at[d - 2], csrc_s, csrc_r
        if d < 2:
            return (
                ke.at[pl.ds(2 if d == 0 else PB, 2), mid], ke.at[pl.ds(PB + 2 if d == 0 else 0, 2), mid],
                ke.at[pl.ds(0 if d == 0 else PB + 2, 2), mid], halo_s, halo_r,
            )
        if d < 4:
            return col_s.at[d - 2], col_r.at[back - 2], col_r.at[d - 2], halo_s, halo_r
        return cor_s.at[d - 4], cor_r.at[back - 4], cor_r.at[d - 4], halo_s, halo_r

    def halo_start(d, kind):
        exists, there = neighbour(d)
        src, dst, _, s_sem, r_sem = halo_copy(d, kind)

        @pl.when(exists)
        def _():
            pltpu.make_async_remote_copy(
                src_ref=src, dst_ref=dst, send_sem=s_sem.at[d], recv_sem=r_sem.at[OPPOSITE[d]], device_id=there,
                device_id_type=LOGICAL,
            ).start()

    def halo_wait(d, kind, then):
        exists, there = neighbour(d)
        src, _, here, s_sem, r_sem = halo_copy(d, kind)

        @pl.when(exists)
        def _():
            copy = pltpu.make_async_remote_copy(
                src_ref=src, dst_ref=here, send_sem=s_sem.at[d], recv_sem=r_sem.at[d], device_id=there,
                device_id_type=LOGICAL,
            )
            copy.wait_send()
            copy.wait_recv()
            then(d)

    for d in range(4):
        halo_start(d, "source")
        halo_start(d, "coarse")

    third = core * 128 + place // 2
    third_f = third.astype(F32)
    weight = jnp.where(third == 0, 1.0, 2.0)
    damp = weight / (1.0 + (2.0 * math.pi * CORRELATION) ** 2 * (waves[0] + third_f * third_f))
    amp = waves[1] * damp
    amp_c = waves[2] * damp
    loads[5].wait()

    def copies_of(send, got, s_sem, r_sem, count):
        some = pl.ds(0, count)
        return pltpu.make_async_remote_copy(
            src_ref=send.at[some], dst_ref=got.at[some], send_sem=s_sem, recv_sem=r_sem, device_id=me,
            device_id_type=LOGICAL,
        )

    z = None
    for i in range(4):
        copies_of(send_f, recv_f, fwd_s, fwd_r.at[i], 64 if i < 3 else 63).wait_recv()
        y4 = lax.rem(my_y + 4 - FAR[i], 4)
        columns = pl.ds(pl.multiple_of(y4 * LANES, LANES), LANES)
        high, low = halves(recv_f[pl.ds(y4 * 64, 64)].reshape(LANES, LANES))
        both = dot(wide[pl.ds(2 * size, size), columns], jnp.concatenate([high, low], axis=1))
        term = both[:, :LANES] + (both[:, LANES:] + dot(wide[pl.ds(3 * size, size), columns], high))
        z = term if z is None else z + term
    z_re, z_im = z[:DEVICES], z[DEVICES:]
    cos, sin = twist[0][...], twist[1][...]
    turned = jnp.concatenate([z_re * cos + z_im * sin, z_im * cos - z_re * sin], axis=1)
    y = table_right(turned, inner)
    x = table_right(y * jnp.concatenate([amp, amp], axis=1), inner_t)
    x_re, x_im = x[:, :LANES], x[:, LANES:]
    xc = table_right(y * jnp.concatenate([amp_c, amp_c], axis=1), inner_c)
    xc_re, xc_im = xc[:, :LANES], xc[:, LANES:]
    cos_c, sin_c = twist_c[0][...], twist_c[1][...]
    fine_part = jnp.concatenate([x_re * cos - x_im * sin, x_im * cos + x_re * sin], axis=0)
    coarse_part = jnp.concatenate([xc_re * cos_c - xc_im * sin_c, xc_im * cos_c + xc_re * sin_c], axis=0)
    high, low = halves(jnp.concatenate([fine_part, coarse_part], axis=1))

    def push_back(i, there, device):
        pltpu.make_async_remote_copy(
            src_ref=send_i.at[there], dst_ref=recv_i.at[place], send_sem=inv_s, recv_sem=inv_r.at[i],
            device_id=device, device_id_type=LOGICAL,
        ).start()

    coarse_place = place // 2

    def push_coarse(i, there, device):
        pltpu.make_async_remote_copy(
            src_ref=send_c.at[there], dst_ref=recv_c.at[coarse_place], send_sem=crs_sem.at[0],
            recv_sem=crs_sem.at[1], device_id=device, device_id_type=LOGICAL,
        ).start()

    for i in range(4):
        y4 = lax.rem(my_y + FAR[i], 4)
        upper = wide[pl.ds(4 * size + y4 * LANES, LANES)]
        lower = wide[pl.ds(5 * size + y4 * LANES, LANES)]
        planes = dot(upper, high) + (dot(upper, low) + dot(lower, high))
        send_i[pl.ds(y4 * 64, 64)] = planes[:, :LANES].reshape(64, 2, LANES)
        send_c[pl.ds(y4 * 64, 64)] = planes[:, LANES:].reshape(64, 2, LANES)
        for_quarter(i, push_back)
    recv_i[place] = send_i[place]

    @pl.when(core == 0)
    def _():
        for_all_peers(push_coarse)
        recv_c[coarse_place] = send_c[place]

    def put_source(d):
        if d >= 2:
            at = EDGE - 1 if d == 2 else EDGE + QB
            for plane in range(PB):
                fe[1 + plane, pl.ds(at, 1)] = scol_r[d - 2, plane]

    def put_coarse(d):
        if d >= 2:
            at = EDGE - 1 if d == 2 else EDGE + half_q
            for plane in range(half_p):
                fc[1 + plane, pl.ds(at, 1)] = cscol_r[d - 2, plane]

    def put_kappa(d):
        dr, dc = DIRECTIONS[d]
        if d >= 4:
            ke[1 if dr < 0 else PB + 2, pl.ds(EDGE - 1 if dc < 0 else EDGE + QB, 1)] = cor_r[d - 4]
        elif d >= 2:
            at = EDGE - 2 if d == 2 else EDGE + QB
            for plane in range(PB):
                ke[2 + plane, pl.ds(at, 2)] = col_r[d - 2, plane]

    for d in range(4):
        halo_wait(d, "source", put_source)
        halo_wait(d, "coarse", put_coarse)
    copies_of(send_f, recv_f, fwd_s, fwd_r.at[0], DEVICES - 1).wait_send()

    fine_log = None
    for i in range(4):
        copies_of(send_i, recv_i, inv_s, inv_r.at[i], 64 if i < 3 else 63).wait_recv()
        y4 = lax.rem(my_y + 4 - FAR[i], 4)
        high, low = halves(recv_i[pl.ds(y4 * 64, 64)].reshape(LANES, LANES).T)
        upper, lower = wide[pl.ds(y4 * LANES, LANES)], wide[pl.ds(size + y4 * LANES, LANES)]
        both = dot(jnp.concatenate([high, low], axis=0), upper)
        term = both[:LANES] + (both[LANES:] + dot(high, lower))
        fine_log = term if fine_log is None else fine_log + term
    fine_kappa = jnp.exp(fine_log).reshape(PB, QB, N2)
    for i, (dr, dc) in enumerate(DIRECTIONS[4:]):
        cor_s[i, 0] = fine_kappa[0 if dr < 0 else PB - 1, 0 if dc < 0 else QB - 1]
    col_s[0] = fine_kappa[:, 0:2]
    col_s[1] = fine_kappa[:, QB - 2 : QB]
    ke[pl.ds(2, PB), mid] = fine_kappa
    for d in (4, 5, 6, 7, 2, 3, 0, 1):
        halo_start(d, "kappa")

    for own in range(2):

        @pl.when(core == own)
        def _(own=own):
            copies_of(recv_c, recv_c, crs_sem.at[0], crs_sem.at[1], 127 + own).wait_recv()

    coarse_log = table_right(recv_c[...].reshape(DEVICES, LANES).T, coarse_third)
    cell = lax.broadcasted_iota(jnp.int32, (LANES, half_n), 0)
    n0 = row * half_p + lax.div(cell, CQ) - 2
    n1 = group * half_q + lax.rem(cell, CQ) - 2
    inside = (n0 >= 0) & (n0 < N0 // 2) & (n1 >= 0) & (n1 < N1 // 2)
    coarse_kappa = jnp.where(inside, jnp.exp(coarse_log), 0.0)
    for plane in range(CP):
        kc[plane, pl.ds(EDGE - 2, CQ)] = coarse_kappa[plane * CQ : (plane + 1) * CQ]
    smooth(kc, fc, uc, coarse_out, half_p, half_q)

    for d in (0, 1, 2, 3, 4, 5, 6, 7):
        halo_wait(d, "kappa", put_kappa)
    smooth(ke, fe, ue, fine_out, PB, QB)

    copies_of(send_i, recv_i, inv_s, inv_r.at[0], DEVICES - 1).wait_send()

    @pl.when(core == 0)
    def _():
        copies_of(send_c, send_c, crs_sem.at[0], crs_sem.at[1], DEVICES - 1).wait_send()


def hand_over(fine, coarse, fine_out, coarse_out):
    fine_out[...] = fine[...]
    coarse_out[...] = coarse[...]


def body(noise, source):
    constants = tables()
    vmem, anywhere = pl.BlockSpec(memory_space=pltpu.VMEM), pl.BlockSpec(memory_space=pl.ANY)
    half_p, half_q, half_n = PB // 2, QB // 2, N2 // 2
    message = pltpu.VMEM((DEVICES, 2, LANES), F32)
    sems = pltpu.SemaphoreType.DMA
    pressures = pl.pallas_call(
        kernel,
        out_shape=(pltpu.VMEM((PB, QB, N2), F32), pltpu.VMEM((half_p, half_q, half_n), F32)),
        in_specs=[anywhere] * 5,
        out_specs=(vmem, vmem),
        scratch_shapes=[pltpu.VMEM((PB, QB, N2), BF16)] * 2
        + [pltpu.VMEM(table.shape, table.dtype) for table in constants]
        + [message] * 5
        + [pltpu.VMEM((128, 2, LANES), F32)]
        + [
            pltpu.VMEM((PB + 4, QB + 16, N2), F32), pltpu.VMEM((PB + 2, QB + 16, N2), F32),
            pltpu.VMEM((PB + 2, QB + 16, N2), F32),
            pltpu.VMEM((half_p + 4, half_q + 16, half_n), F32), pltpu.VMEM((half_p + 2, half_q + 16, half_n), F32),
            pltpu.VMEM((half_p + 2, half_q + 16, half_n), F32),
        ]
        + [pltpu.VMEM((2, PB, 2, N2), F32)] * 2
        + [pltpu.VMEM((4, 1, N2), F32)] * 2
        + [pltpu.VMEM((2, PB, 1, N2), F32)] * 2
        + [pltpu.VMEM((2, half_p, 1, half_n), F32)] * 2
        + [sems((6,)), sems, sems((4,)), sems, sems((4,)), sems((2,))]
        + [sems((8,))] * 2
        + [sems((4,))] * 4,
        compiler_params=pltpu.CompilerParams(collective_id=0, has_side_effects=True, vmem_limit_bytes=VMEM_LIMIT),
    )(noise, source, *[jnp.asarray(table) for table in constants])
    return pl.pallas_call(
        hand_over,
        out_shape=tuple(jax.ShapeDtypeStruct(value.shape, value.dtype) for value in pressures),
        in_specs=[vmem] * 2,
        out_specs=(vmem, vmem),
        compiler_params=pltpu.CompilerParams(vmem_limit_bytes=2 << 20),
    )(*pressures)


def solution(mesh):
    return jax.shard_map(
        body,
        mesh=mesh,
        in_specs=(P("row", ("level", "col"), None), P("row", ("level", "col"), None)),
        out_specs=(P("row", ("level", "col"), None), P("row", ("level", "col"), None)),
        check_vma=False,
    )
```

```python
import functools
import math

import jax
import jax.numpy as jnp
import ml_dtypes
import numpy as np
from jax import lax
from jax.experimental import pallas as pl
from jax.experimental.pallas import tpu as pltpu
from jax.sharding import PartitionSpec as P

JACOBI_WEIGHT = 2.0 / 3.0
CORRELATION = 0.2
FIELD_SCALE = 0.3
LOGICAL = pl.DeviceIdType.LOGICAL
F32 = jnp.float32
BF16 = jnp.bfloat16

N0, N1, N2 = 64, 512, 512
ROWS, COLS = 16, 16
DEVICES = ROWS * COLS
PB, QB = N0 // ROWS, N1 // COLS
LANES = PB * QB
CP, CQ = PB // 2 + 4, QB // 2 + 4
CELLS = CP * CQ
VMEM_LIMIT = 60 << 20
FAR = (2, 1, 3, 0)
EDGE = 8


def split_table(table):
    high = table.astype(ml_dtypes.bfloat16)
    low = (table - high.astype(np.float64)).astype(ml_dtypes.bfloat16)
    return high, low


def signed(index, length):
    return np.where(index < length // 2, index, index - length).astype(np.float64)


def columns_of(column):
    y, x = column // 4, column % 4
    return (x % 2) * 8 + y * 2 + x // 2


@functools.lru_cache(maxsize=None)
def tables():
    place = np.arange(DEVICES)
    r, c = place % ROWS, columns_of(place // ROWS)
    third = (r % 2) * 128 + place // 2
    turn = 2.0 * np.pi
    n2 = np.arange(N2)
    angle = turn * ((third[:, None] * n2[None, :]) % N2) / N2
    third_table = np.stack([np.cos(angle), -np.sin(angle)], axis=1).reshape(2 * DEVICES, N2)
    k2 = np.arange(128)
    angle = turn * ((k2[:, None] * np.arange(N2 // 2)[None, :]) % (N2 // 2)) / (N2 // 2)
    coarse_third = np.stack([np.cos(angle), -np.sin(angle)], axis=1).reshape(256, N2 // 2)
    a, b = place // 16, place % 16
    angle = turn * ((a[:, None] * r[None, :] + b[:, None] * c[None, :]) % 16) / 16
    cos, sin = np.cos(angle), np.sin(angle)
    outer = np.concatenate([np.stack([cos, sin], axis=2), np.stack([-sin, cos], axis=2)], axis=0)
    outer = outer.reshape(2 * DEVICES, 2 * DEVICES)
    lane = np.arange(LANES)
    p, q = lane // QB, lane % QB
    angle = turn * (((8 * p[:, None] * p[None, :]) + q[:, None] * q[None, :]) % 32) / 32
    cos, sin = np.cos(angle), np.sin(angle)
    inner = np.block([[cos, -sin], [sin, cos]])
    lane_c = np.arange(CELLS)
    pc, qc = lane_c // CQ - 2, lane_c % CQ - 2
    angle = turn * (((8 * p[:, None] * pc[None, :]) + q[:, None] * qc[None, :]) % 16) / 16
    cos, sin = np.cos(angle), np.sin(angle)
    empty = np.zeros((LANES, LANES - CELLS))
    inner_c = np.block([[cos, empty, sin, empty], [-sin, empty, cos, empty]])
    angle = turn * ((8 * a[:, None] * p[None, :] + b[:, None] * q[None, :]) % 512) / 512
    twist = np.stack([np.cos(angle), np.sin(angle)])
    angle = turn * ((8 * a[:, None] * pc[None, :] + b[:, None] * qc[None, :]) % 256) / 256
    rest = np.zeros((DEVICES, LANES - CELLS))
    twist_c = np.stack([np.concatenate([np.cos(angle), rest], 1), np.concatenate([np.sin(angle), rest], 1)])
    m0 = signed(a[:, None] + 16 * p[None, :], N0)
    m1 = signed(b[:, None] + 16 * q[None, :], N1)
    norm = (float(N0) * N1 * N2) ** -0.5
    inside = (m0 != -N0 // 2) & (m1 != -N1 // 2)
    inside_c = (np.abs(m0) < N0 // 4) & (np.abs(m1) < N1 // 4)
    waves = np.stack([m0 * m0 + m1 * m1, inside * FIELD_SCALE * norm, inside_c * FIELD_SCALE * norm])
    pool = (np.arange(N2)[:, None] // 2 == np.arange(N2 // 2)[None, :]).astype(ml_dtypes.bfloat16)
    pool_rows = (np.arange(32)[:, None] == ((p // 2) * 16 + q // 2)[None, :]) * 0.125
    pool_rows = np.concatenate([pool_rows, np.zeros((32, LANES))], axis=1).astype(ml_dtypes.bfloat16)
    wide = np.concatenate([part for table in (third_table, outer, outer.T) for part in split_table(table)])
    narrow = np.concatenate([part for table in (inner, inner.T, inner_c, coarse_third) for part in split_table(table)])
    narrow = np.concatenate([narrow, pool, pool_rows])
    return wide, narrow, np.concatenate([twist, twist_c, waves]).astype(np.float32)


def halves(value):
    high = value.astype(BF16)
    return high, (value - high.astype(F32)).astype(BF16)


def dot(left, right):
    return jnp.dot(left, right, preferred_element_type=F32)


def table_right(value, table):
    high, low = halves(value)
    return dot(high, table[0]) + (dot(high, table[1]) + dot(low, table[0]))


DIRECTIONS = ((-1, 0), (1, 0), (0, -1), (0, 1), (-1, -1), (-1, 1), (1, -1), (1, 1))
OPPOSITE = (1, 0, 3, 2, 7, 6, 5, 4)


def flat_id(r, c):
    return (c // 8) * 128 + r * 8 + c % 8


def beside_lanes(value):
    depth = value.shape[-1]
    lane = lax.broadcasted_iota(jnp.int32, value.shape, 1)
    after = jnp.where(lane == depth - 1, 0.0, pltpu.roll(value, depth - 1, 1))
    before = jnp.where(lane == 0, 0.0, pltpu.roll(value, 1, 1))
    return after, before


def first_sweep(half, neighbours, source):
    diagonal = 6.0 * half
    for beside in neighbours:
        diagonal = diagonal + jnp.where(beside > 0.0, beside, half)
    return JACOBI_WEIGHT * source / jnp.where(half > 0.0, diagonal, 1.0), diagonal


def smooth(halved, source, first, out, planes, width):
    mid, low, high = pl.ds(EDGE, width), pl.ds(EDGE - 1, width), pl.ds(EDGE + 1, width)
    for plane in range(planes + 2):
        half = halved[plane + 1, mid]
        near = (halved[plane + 2, mid], halved[plane, mid], halved[plane + 1, high], halved[plane + 1, low])
        value, diagonal = first_sweep(half, near + beside_lanes(half), source[plane, mid])
        first[plane, mid] = value
        if 1 <= plane <= planes:
            out[plane - 1] = diagonal
    for at, inward, outward in ((EDGE - 1, EDGE, EDGE - 2), (EDGE + width, EDGE + width - 1, EDGE + width + 1)):

        def line(ref, base, q):
            return jnp.concatenate([ref[base + plane, pl.ds(q, 1)] for plane in range(planes)], axis=0)

        half = line(halved, 2, at)
        near = (line(halved, 3, at), line(halved, 1, at), line(halved, 2, inward), line(halved, 2, outward))
        value, _ = first_sweep(half, near + beside_lanes(half), line(source, 1, at))
        for plane in range(planes):
            first[1 + plane, pl.ds(at, 1)] = value[plane : plane + 1]
    for plane in range(planes):
        half = halved[plane + 2, mid]
        inner = first[plane + 1, mid]
        diagonal = out[plane]
        total = source[plane + 1, mid] - diagonal * inner
        after, before = beside_lanes(half)
        after_value, before_value = beside_lanes(inner)
        for beside, value in (
            (halved[plane + 3, mid], first[plane + 2, mid]),
            (halved[plane + 1, mid], first[plane, mid]),
            (halved[plane + 2, high], first[plane + 1, high]),
            (halved[plane + 2, low], first[plane + 1, low]),
            (after, after_value),
            (before, before_value),
        ):
            total = total + (half + jnp.where(beside > 0.0, beside, half)) * value
        out[plane] = inner + JACOBI_WEIGHT * total / diagonal


def kernel(
    noise_h, source_h, wide_h, narrow_h, tables_h, fine_out, coarse_out,
    noise, source, wide, narrow, tables_v,
    send_f, recv_f, send_i, recv_i, send_c, recv_c,
    ke, fe, ue, kc, fc, uc,
    col_s, col_r, cor_s, cor_r, scol_s, scol_r, cscol_s, cscol_r,
    table_sem, fwd_s, fwd_r, inv_s, inv_r, crs_sem, halo_s, halo_r, src_s, src_r, csrc_s, csrc_r,
):
    level, row, col = lax.axis_index("level"), lax.axis_index("row"), lax.axis_index("col")
    group = level * 8 + col
    me = flat_id(row, group)
    core, my_z = lax.rem(row, 2), row // 2
    my_y, my_x = col // 2, lax.rem(col, 2) * 2 + level
    place = (my_y * 4 + my_x) * ROWS + row
    half_p, half_q, half_n = PB // 2, QB // 2, N2 // 2

    rows = []
    for step in (4, 3, 5, 2, 6, 1, 7, 0):
        z2 = lax.rem(my_z + step, 8) * 2
        rows += [z2 + 1 - core, z2 + core]
    rows = [(r, r * 8) for r in rows]

    def far(j):
        return 2 + (1 - 2 * lax.rem(j, 2)) * ((j + 1) // 2)

    def for_column(i, j, step, count=ROWS):
        y, x = lax.rem(my_y + FAR[i], 4), lax.rem(my_x + far(j), 4)
        first, part = (y * 4 + x) * ROWS, lax.rem(x, 2) * 128 + y * 2 + x // 2
        for r, r8 in rows[:count]:
            step(i, first + r, part + r8)

    def for_quarter(i, step):
        def one(j, carry):
            for_column(i, j, step)
            return carry

        if i < 3:
            lax.fori_loop(0, 4, one, 0)
        else:
            lax.fori_loop(0, 3, one, 0)
            for_column(3, 3, step, ROWS - 1)

    def for_all_peers(step):
        for i in range(4):
            for_quarter(i, step)

    barrier = pltpu.get_barrier_semaphore()

    def greet(i, there, device):
        pl.semaphore_signal(barrier, inc=1, device_id=device, device_id_type=LOGICAL)


    size = 2 * DEVICES
    pairs = (
        (noise_h, noise), (source_h, source),
        (wide_h.at[pl.ds(0, 2 * size)], wide.at[pl.ds(0, 2 * size)]),
        (narrow_h, narrow), (tables_h, tables_v),
        (wide_h.at[pl.ds(2 * size, 4 * size)], wide.at[pl.ds(2 * size, 4 * size)]),
    )
    loads = [pltpu.make_async_copy(a, b, table_sem.at[i]) for i, (a, b) in enumerate(pairs)]
    for load in loads[:3]:
        load.start()
    for_all_peers(greet)
    for load in loads[3:]:
        load.start()

    class Parts:
        def __init__(self, ref, at, count):
            self.ref, self.at, self.count = ref, at, count

        def __getitem__(self, part):
            return self.ref[pl.ds(self.at + part * self.count, self.count)]

    third_t = Parts(wide, 0, size)
    inner, inner_t, inner_c, coarse_third = (Parts(narrow, i * size, DEVICES) for i in range(4))
    twist, twist_c, waves = (tables_v.at[0], tables_v.at[1]), (tables_v.at[2], tables_v.at[3]), tables_v.at[pl.ds(4, 3)]

    for ref, width in ((ke, QB), (fe, QB), (fc, half_q)):
        for at in (0, EDGE + width):
            ref[:, pl.ds(at, EDGE)] = jnp.zeros((ref.shape[0], EDGE, ref.shape[2]), F32)

    for edge, last in ((0, False), (ROWS - 1, True)):

        @pl.when(row == edge)
        def _(last=last):
            for ref, width, layers in ((ke, QB, 2), (fe, QB, 1), (fc, half_q, 1)):
                at = ref.shape[0] - layers if last else 0
                ref[pl.ds(at, layers), pl.ds(EDGE, width)] = jnp.zeros((layers, width, ref.shape[2]), F32)

    loads[0].wait()
    loads[1].wait()
    loads[2].wait()
    noise_rows = noise[...].reshape(LANES, N2)
    contract = (((1,), (1,)), ((), ()))
    spectrum = lax.dot_general(third_t[0], noise_rows, contract, preferred_element_type=F32)
    spectrum = spectrum + lax.dot_general(third_t[1], noise_rows, contract, preferred_element_type=F32)
    send_f[...] = spectrum.reshape(DEVICES, 2, LANES)

    fe[pl.ds(1, PB), pl.ds(EDGE, QB)] = source[...].astype(F32)
    scol_s[0, :, 0] = source[:, 0].astype(F32)
    scol_s[1, :, 0] = source[:, QB - 1].astype(F32)

    pl.semaphore_wait(barrier, DEVICES - 1)

    def push(i, there, device):
        pltpu.make_async_remote_copy(
            src_ref=send_f.at[there], dst_ref=recv_f.at[place], send_sem=fwd_s, recv_sem=fwd_r.at[i],
            device_id=device, device_id_type=LOGICAL,
        ).start()

    for_all_peers(push)
    recv_f[place] = send_f[place]

    loads[3].wait()
    loads[4].wait()
    high, low = halves(dot(narrow[pl.ds(5 * size, 32), pl.ds(0, LANES)], source[...].reshape(LANES, N2)))
    pool = narrow[pl.ds(4 * size, size)]
    pooled = (dot(high, pool) + dot(low, pool)).reshape(half_p, half_q, half_n)
    fc[pl.ds(1, half_p), pl.ds(EDGE, half_q)] = pooled
    cscol_s[0, :, 0] = pooled[:, 0]
    cscol_s[1, :, 0] = pooled[:, half_q - 1]

    def neighbour(d):
        dr, dc = DIRECTIONS[d]
        r, c = row + dr, group + dc
        exists = (r >= 0) & (r < ROWS) & (c >= 0) & (c < COLS)
        return exists, flat_id(r, c)

    mid, mid_c = pl.ds(EDGE, QB), pl.ds(EDGE, half_q)

    def halo_copy(d, kind):
        back = OPPOSITE[d]
        if kind == "source":
            if d < 2:
                return (
                    fe.at[1 if d == 0 else PB, mid], fe.at[PB + 1 if d == 0 else 0, mid],
                    fe.at[0 if d == 0 else PB + 1, mid], src_s, src_r,
                )
            return scol_s.at[d - 2], scol_r.at[back - 2], scol_r.at[d - 2], src_s, src_r
        if kind == "coarse":
            if d < 2:
                return (
                    fc.at[1 if d == 0 else half_p, mid_c], fc.at[half_p + 1 if d == 0 else 0, mid_c],
                    fc.at[0 if d == 0 else half_p + 1, mid_c], csrc_s, csrc_r,
                )
            return cscol_s.at[d - 2], cscol_r.at[back - 2], cscol_r.at[d - 2], csrc_s, csrc_r
        if d < 2:
            return (
                ke.at[pl.ds(2 if d == 0 else PB, 2), mid], ke.at[pl.ds(PB + 2 if d == 0 else 0, 2), mid],
                ke.at[pl.ds(0 if d == 0 else PB + 2, 2), mid], halo_s, halo_r,
            )
        if d < 4:
            return col_s.at[d - 2], col_r.at[back - 2], col_r.at[d - 2], halo_s, halo_r
        return cor_s.at[d - 4], cor_r.at[back - 4], cor_r.at[d - 4], halo_s, halo_r

    def halo_start(d, kind):
        exists, there = neighbour(d)
        src, dst, _, s_sem, r_sem = halo_copy(d, kind)

        @pl.when(exists)
        def _():
            pltpu.make_async_remote_copy(
                src_ref=src, dst_ref=dst, send_sem=s_sem.at[d], recv_sem=r_sem.at[OPPOSITE[d]], device_id=there,
                device_id_type=LOGICAL,
            ).start()

    def halo_wait(d, kind, then):
        exists, there = neighbour(d)
        src, _, here, s_sem, r_sem = halo_copy(d, kind)

        @pl.when(exists)
        def _():
            copy = pltpu.make_async_remote_copy(
                src_ref=src, dst_ref=here, send_sem=s_sem.at[d], recv_sem=r_sem.at[d], device_id=there,
                device_id_type=LOGICAL,
            )
            copy.wait_send()
            copy.wait_recv()
            then(d)

    for d in range(4):
        halo_start(d, "source")
        halo_start(d, "coarse")

    third = core * 128 + place // 2
    third_f = third.astype(F32)
    weight = jnp.where(third == 0, 1.0, 2.0)
    damp = weight / (1.0 + (2.0 * math.pi * CORRELATION) ** 2 * (waves[0] + third_f * third_f))
    amp = waves[1] * damp
    amp_c = waves[2] * damp
    loads[5].wait()

    def copies_of(send, got, s_sem, r_sem, count):
        some = pl.ds(0, count)
        return pltpu.make_async_remote_copy(
            src_ref=send.at[some], dst_ref=got.at[some], send_sem=s_sem, recv_sem=r_sem, device_id=me,
            device_id_type=LOGICAL,
        )

    z = None
    for i in range(4):
        copies_of(send_f, recv_f, fwd_s, fwd_r.at[i], 64 if i < 3 else 63).wait_recv()
        y4 = lax.rem(my_y + 4 - FAR[i], 4)
        columns = pl.ds(pl.multiple_of(y4 * LANES, LANES), LANES)
        high, low = halves(recv_f[pl.ds(y4 * 64, 64)].reshape(LANES, LANES))
        both = dot(wide[pl.ds(2 * size, size), columns], jnp.concatenate([high, low], axis=1))
        term = both[:, :LANES] + (both[:, LANES:] + dot(wide[pl.ds(3 * size, size), columns], high))
        z = term if z is None else z + term
    z_re, z_im = z[:DEVICES], z[DEVICES:]
    cos, sin = twist[0][...], twist[1][...]
    turned = jnp.concatenate([z_re * cos + z_im * sin, z_im * cos - z_re * sin], axis=1)
    y = table_right(turned, inner)
    x = table_right(y * jnp.concatenate([amp, amp], axis=1), inner_t)
    x_re, x_im = x[:, :LANES], x[:, LANES:]
    fine_part = jnp.concatenate([x_re * cos - x_im * sin, x_im * cos + x_re * sin], axis=0)
    high, low = halves(fine_part)
    high_low = jnp.concatenate([high, low], axis=1)

    def push_back(i, there, device):
        pltpu.make_async_remote_copy(
            src_ref=send_i.at[there], dst_ref=recv_i.at[place], send_sem=inv_s, recv_sem=inv_r.at[i],
            device_id=device, device_id_type=LOGICAL,
        ).start()

    coarse_place = place // 2

    def push_coarse(i, there, device):
        pltpu.make_async_remote_copy(
            src_ref=send_c.at[there], dst_ref=recv_c.at[coarse_place], send_sem=crs_sem.at[0],
            recv_sem=crs_sem.at[1], device_id=device, device_id_type=LOGICAL,
        ).start()

    for i in range(4):
        y4 = lax.rem(my_y + FAR[i], 4)
        upper = wide[pl.ds(4 * size + y4 * LANES, LANES)]
        lower = wide[pl.ds(5 * size + y4 * LANES, LANES)]
        both = dot(upper, high_low)
        planes = both[:, :LANES] + (both[:, LANES:] + dot(lower, high))
        send_i[pl.ds(y4 * 64, 64)] = planes.reshape(64, 2, LANES)
        for_quarter(i, push_back)
    recv_i[place] = send_i[place]

    @pl.when(core == 0)
    def _():
        xc = table_right(y * jnp.concatenate([amp_c, amp_c], axis=1), inner_c)
        xc_re, xc_im = xc[:, :LANES], xc[:, LANES:]
        cos_c, sin_c = twist_c[0][...], twist_c[1][...]
        high, low = halves(jnp.concatenate([xc_re * cos_c - xc_im * sin_c, xc_im * cos_c + xc_re * sin_c], axis=0))
        high_low = jnp.concatenate([high, low], axis=1)
        for i in range(4):
            y4 = lax.rem(my_y + FAR[i], 4)
            upper = wide[pl.ds(4 * size + y4 * LANES, LANES)]
            lower = wide[pl.ds(5 * size + y4 * LANES, LANES)]
            both = dot(upper, high_low)
            planes = both[:, :LANES] + (both[:, LANES:] + dot(lower, high))
            send_c[pl.ds(y4 * 64, 64)] = planes.reshape(64, 2, LANES)
            for_quarter(i, push_coarse)
        recv_c[coarse_place] = send_c[place]

    def put_source(d):
        if d >= 2:
            at = EDGE - 1 if d == 2 else EDGE + QB
            for plane in range(PB):
                fe[1 + plane, pl.ds(at, 1)] = scol_r[d - 2, plane]

    def put_coarse(d):
        if d >= 2:
            at = EDGE - 1 if d == 2 else EDGE + half_q
            for plane in range(half_p):
                fc[1 + plane, pl.ds(at, 1)] = cscol_r[d - 2, plane]

    def put_kappa(d):
        dr, dc = DIRECTIONS[d]
        if d >= 4:
            ke[1 if dr < 0 else PB + 2, pl.ds(EDGE - 1 if dc < 0 else EDGE + QB, 1)] = cor_r[d - 4]
        elif d >= 2:
            at = EDGE - 2 if d == 2 else EDGE + QB
            for plane in range(PB):
                ke[2 + plane, pl.ds(at, 2)] = col_r[d - 2, plane]

    for d in range(4):
        halo_wait(d, "source", put_source)
        halo_wait(d, "coarse", put_coarse)
    copies_of(send_f, recv_f, fwd_s, fwd_r.at[0], DEVICES - 1).wait_send()

    fine_log = None
    for i in range(4):
        copies_of(send_i, recv_i, inv_s, inv_r.at[i], 64 if i < 3 else 63).wait_recv()
        y4 = lax.rem(my_y + 4 - FAR[i], 4)
        high, low = halves(recv_i[pl.ds(y4 * 64, 64)].reshape(LANES, LANES).T)
        upper, lower = wide[pl.ds(y4 * LANES, LANES)], wide[pl.ds(size + y4 * LANES, LANES)]
        both = dot(jnp.concatenate([high, low], axis=0), upper)
        term = both[:LANES] + (both[LANES:] + dot(high, lower))
        fine_log = term if fine_log is None else fine_log + term
    fine_half = (0.5 * jnp.exp(fine_log)).reshape(PB, QB, N2)
    for i, (dr, dc) in enumerate(DIRECTIONS[4:]):
        cor_s[i, 0] = fine_half[0 if dr < 0 else PB - 1, 0 if dc < 0 else QB - 1]
    col_s[0] = fine_half[:, 0:2]
    col_s[1] = fine_half[:, QB - 2 : QB]
    ke[pl.ds(2, PB), mid] = fine_half
    for d in (4, 5, 6, 7, 2, 3, 0, 1):
        halo_start(d, "kappa")

    for own in range(2):

        @pl.when(core == own)
        def _(own=own):
            copies_of(recv_c, recv_c, crs_sem.at[0], crs_sem.at[1], 127 + own).wait_recv()

    coarse_log = table_right(recv_c[...].reshape(DEVICES, LANES).T, coarse_third)
    cell = lax.broadcasted_iota(jnp.int32, (LANES, half_n), 0)
    n0 = row * half_p + lax.div(cell, CQ) - 2
    n1 = group * half_q + lax.rem(cell, CQ) - 2
    inside = (n0 >= 0) & (n0 < N0 // 2) & (n1 >= 0) & (n1 < N1 // 2)
    coarse_half = jnp.where(inside, 0.5 * jnp.exp(coarse_log), 0.0)
    for plane in range(CP):
        kc[plane, pl.ds(EDGE - 2, CQ)] = coarse_half[plane * CQ : (plane + 1) * CQ]
    smooth(kc, fc, uc, coarse_out, half_p, half_q)

    for d in (0, 1, 2, 3, 4, 5, 6, 7):
        halo_wait(d, "kappa", put_kappa)
    smooth(ke, fe, ue, fine_out, PB, QB)

    copies_of(send_i, recv_i, inv_s, inv_r.at[0], DEVICES - 1).wait_send()

    @pl.when(core == 0)
    def _():
        copies_of(send_c, send_c, crs_sem.at[0], crs_sem.at[1], DEVICES - 1).wait_send()


def hand_over(fine, coarse, fine_out, coarse_out):
    fine_out[...] = fine[...]
    coarse_out[...] = coarse[...]


def body(noise, source):
    constants = tables()
    vmem, anywhere = pl.BlockSpec(memory_space=pltpu.VMEM), pl.BlockSpec(memory_space=pl.ANY)
    half_p, half_q, half_n = PB // 2, QB // 2, N2 // 2
    message = pltpu.VMEM((DEVICES, 2, LANES), F32)
    sems = pltpu.SemaphoreType.DMA
    pressures = pl.pallas_call(
        kernel,
        out_shape=(pltpu.VMEM((PB, QB, N2), F32), pltpu.VMEM((half_p, half_q, half_n), F32)),
        in_specs=[anywhere] * 5,
        out_specs=(vmem, vmem),
        scratch_shapes=[pltpu.VMEM((PB, QB, N2), BF16)] * 2
        + [pltpu.VMEM(table.shape, table.dtype) for table in constants]
        + [message] * 5
        + [pltpu.VMEM((128, 2, LANES), F32)]
        + [
            pltpu.VMEM((PB + 4, QB + 16, N2), F32), pltpu.VMEM((PB + 2, QB + 16, N2), F32),
            pltpu.VMEM((PB + 2, QB + 16, N2), F32),
            pltpu.VMEM((half_p + 4, half_q + 16, half_n), F32), pltpu.VMEM((half_p + 2, half_q + 16, half_n), F32),
            pltpu.VMEM((half_p + 2, half_q + 16, half_n), F32),
        ]
        + [pltpu.VMEM((2, PB, 2, N2), F32)] * 2
        + [pltpu.VMEM((4, 1, N2), F32)] * 2
        + [pltpu.VMEM((2, PB, 1, N2), F32)] * 2
        + [pltpu.VMEM((2, half_p, 1, half_n), F32)] * 2
        + [sems((6,)), sems, sems((4,)), sems, sems((4,)), sems((2,))]
        + [sems((8,))] * 2
        + [sems((4,))] * 4,
        compiler_params=pltpu.CompilerParams(collective_id=0, has_side_effects=True, vmem_limit_bytes=VMEM_LIMIT),
    )(noise, source, *[jnp.asarray(table) for table in constants])
    return pl.pallas_call(
        hand_over,
        out_shape=tuple(jax.ShapeDtypeStruct(value.shape, value.dtype) for value in pressures),
        in_specs=[vmem] * 2,
        out_specs=(vmem, vmem),
        compiler_params=pltpu.CompilerParams(vmem_limit_bytes=2 << 20),
    )(*pressures)


def solution(mesh):
    return jax.shard_map(
        body,
        mesh=mesh,
        in_specs=(P("row", ("level", "col"), None), P("row", ("level", "col"), None)),
        out_specs=(P("row", ("level", "col"), None), P("row", ("level", "col"), None)),
        check_vma=False,
    )
```

```python
import functools
import math

import jax
import jax.numpy as jnp
import ml_dtypes
import numpy as np
from jax import lax
from jax.experimental import pallas as pl
from jax.experimental.pallas import tpu as pltpu
from jax.sharding import PartitionSpec as P

JACOBI_WEIGHT = 2.0 / 3.0
CORRELATION = 0.2
FIELD_SCALE = 0.3
LOGICAL = pl.DeviceIdType.LOGICAL
F32 = jnp.float32
BF16 = jnp.bfloat16

N0, N1, N2 = 64, 512, 512
ROWS, COLS = 16, 16
DEVICES = ROWS * COLS
PB, QB = N0 // ROWS, N1 // COLS
LANES = PB * QB
CP, CQ = PB // 2 + 4, QB // 2 + 4
CELLS = CP * CQ
VMEM_LIMIT = 60 << 20
FAR = (2, 1, 3, 0)
EDGE = 8


def split_table(table):
    high = table.astype(ml_dtypes.bfloat16)
    low = (table - high.astype(np.float64)).astype(ml_dtypes.bfloat16)
    return high, low


def signed(index, length):
    return np.where(index < length // 2, index, index - length).astype(np.float64)


def columns_of(column):
    y, x = column // 4, column % 4
    return (x % 2) * 8 + y * 2 + x // 2


@functools.lru_cache(maxsize=None)
def tables():
    place = np.arange(DEVICES)
    r, c = place % ROWS, columns_of(place // ROWS)
    third = (r % 2) * 128 + place // 2
    turn = 2.0 * np.pi
    n2 = np.arange(N2)
    angle = turn * ((third[:, None] * n2[None, :]) % N2) / N2
    third_table = np.stack([np.cos(angle), -np.sin(angle)], axis=1).reshape(2 * DEVICES, N2)
    k2 = np.arange(128)
    angle = turn * ((k2[:, None] * np.arange(N2 // 2)[None, :]) % (N2 // 2)) / (N2 // 2)
    coarse_third = np.stack([np.cos(angle), -np.sin(angle)], axis=1).reshape(256, N2 // 2)
    a, b = place // 16, place % 16
    angle = turn * ((a[:, None] * r[None, :] + b[:, None] * c[None, :]) % 16) / 16
    cos, sin = np.cos(angle), np.sin(angle)
    outer = np.concatenate([np.stack([cos, sin], axis=2), np.stack([-sin, cos], axis=2)], axis=0)
    outer = outer.reshape(2 * DEVICES, 2 * DEVICES)
    lane = np.arange(LANES)
    p, q = lane // QB, lane % QB
    angle = turn * (((8 * p[:, None] * p[None, :]) + q[:, None] * q[None, :]) % 32) / 32
    cos, sin = np.cos(angle), np.sin(angle)
    inner = np.block([[cos, -sin], [sin, cos]])
    lane_c = np.arange(CELLS)
    pc, qc = lane_c // CQ - 2, lane_c % CQ - 2
    angle = turn * (((8 * p[:, None] * pc[None, :]) + q[:, None] * qc[None, :]) % 16) / 16
    cos, sin = np.cos(angle), np.sin(angle)
    empty = np.zeros((LANES, LANES - CELLS))
    inner_c = np.block([[cos, empty, sin, empty], [-sin, empty, cos, empty]])
    angle = turn * ((8 * a[:, None] * p[None, :] + b[:, None] * q[None, :]) % 512) / 512
    twist = np.stack([np.cos(angle), np.sin(angle)])
    angle = turn * ((8 * a[:, None] * pc[None, :] + b[:, None] * qc[None, :]) % 256) / 256
    rest = np.zeros((DEVICES, LANES - CELLS))
    twist_c = np.stack([np.concatenate([np.cos(angle), rest], 1), np.concatenate([np.sin(angle), rest], 1)])
    m0 = signed(a[:, None] + 16 * p[None, :], N0)
    m1 = signed(b[:, None] + 16 * q[None, :], N1)
    norm = (float(N0) * N1 * N2) ** -0.5
    inside = (m0 != -N0 // 2) & (m1 != -N1 // 2)
    inside_c = (np.abs(m0) < N0 // 4) & (np.abs(m1) < N1 // 4)
    waves = np.stack([m0 * m0 + m1 * m1, inside * FIELD_SCALE * norm, inside_c * FIELD_SCALE * norm])
    pool = (np.arange(N2)[:, None] // 2 == np.arange(N2 // 2)[None, :]).astype(ml_dtypes.bfloat16)
    pool_rows = (np.arange(32)[:, None] == ((p // 2) * 16 + q // 2)[None, :]) * 0.125
    pool_rows = np.concatenate([pool_rows, np.zeros((32, LANES))], axis=1).astype(ml_dtypes.bfloat16)
    wide = np.concatenate([part for table in (third_table, outer, outer.T) for part in split_table(table)])
    narrow = np.concatenate([part for table in (inner, inner.T, inner_c, coarse_third) for part in split_table(table)])
    narrow = np.concatenate([narrow, pool, pool_rows])
    return wide, narrow, np.concatenate([twist, twist_c, waves]).astype(np.float32)


def halves(value):
    high = value.astype(BF16)
    return high, (value - high.astype(F32)).astype(BF16)


def dot(left, right):
    return jnp.dot(left, right, preferred_element_type=F32)


def table_right(value, table):
    high, low = halves(value)
    return dot(high, table[0]) + (dot(high, table[1]) + dot(low, table[0]))


DIRECTIONS = ((-1, 0), (1, 0), (0, -1), (0, 1), (-1, -1), (-1, 1), (1, -1), (1, 1))
OPPOSITE = (1, 0, 3, 2, 7, 6, 5, 4)


def flat_id(r, c):
    return (c // 8) * 128 + r * 8 + c % 8


def beside_lanes(value):
    depth = value.shape[-1]
    lane = lax.broadcasted_iota(jnp.int32, value.shape, 1)
    after = jnp.where(lane == depth - 1, 0.0, pltpu.roll(value, depth - 1, 1))
    before = jnp.where(lane == 0, 0.0, pltpu.roll(value, 1, 1))
    return after, before


def first_sweep(half, neighbours, source):
    diagonal = 6.0 * half
    for beside in neighbours:
        diagonal = diagonal + jnp.where(beside > 0.0, beside, half)
    return JACOBI_WEIGHT * source / jnp.where(half > 0.0, diagonal, 1.0), diagonal


def smooth(halved, source, first, out, planes, width):
    mid, low, high = pl.ds(EDGE, width), pl.ds(EDGE - 1, width), pl.ds(EDGE + 1, width)
    for plane in range(planes + 2):
        half = halved[plane + 1, mid]
        near = (halved[plane + 2, mid], halved[plane, mid], halved[plane + 1, high], halved[plane + 1, low])
        value, diagonal = first_sweep(half, near + beside_lanes(half), source[plane, mid])
        first[plane, mid] = value
        if 1 <= plane <= planes:
            out[plane - 1] = diagonal
    for at, inward, outward in ((EDGE - 1, EDGE, EDGE - 2), (EDGE + width, EDGE + width - 1, EDGE + width + 1)):

        def line(ref, base, q):
            return jnp.concatenate([ref[base + plane, pl.ds(q, 1)] for plane in range(planes)], axis=0)

        half = line(halved, 2, at)
        near = (line(halved, 3, at), line(halved, 1, at), line(halved, 2, inward), line(halved, 2, outward))
        value, _ = first_sweep(half, near + beside_lanes(half), line(source, 1, at))
        for plane in range(planes):
            first[1 + plane, pl.ds(at, 1)] = value[plane : plane + 1]
    for plane in range(planes):
        half = halved[plane + 2, mid]
        inner = first[plane + 1, mid]
        diagonal = out[plane]
        total = source[plane + 1, mid] - diagonal * inner
        after, before = beside_lanes(half)
        after_value, before_value = beside_lanes(inner)
        for beside, value in (
            (halved[plane + 3, mid], first[plane + 2, mid]),
            (halved[plane + 1, mid], first[plane, mid]),
            (halved[plane + 2, high], first[plane + 1, high]),
            (halved[plane + 2, low], first[plane + 1, low]),
            (after, after_value),
            (before, before_value),
        ):
            total = total + (half + jnp.where(beside > 0.0, beside, half)) * value
        out[plane] = inner + JACOBI_WEIGHT * total / diagonal


def kernel(
    noise_h, source_h, wide_h, narrow_h, tables_h, fine_out, coarse_out,
    noise, source, wide, narrow, tables_v,
    send_f, recv_f, send_i, recv_i, send_c, recv_c,
    ke, fe, ue, kc, fc, uc,
    col_s, col_r, cor_s, cor_r, scol_s, scol_r, cscol_s, cscol_r,
    table_sem, fwd_s, fwd_r, inv_s, inv_r, crs_sem, halo_s, halo_r, src_s, src_r, csrc_s, csrc_r,
):
    level, row, col = lax.axis_index("level"), lax.axis_index("row"), lax.axis_index("col")
    group = level * 8 + col
    me = flat_id(row, group)
    core, my_z = lax.rem(row, 2), row // 2
    my_y, my_x = col // 2, lax.rem(col, 2) * 2 + level
    place = (my_y * 4 + my_x) * ROWS + row
    half_p, half_q, half_n = PB // 2, QB // 2, N2 // 2

    rows = []
    for step in (4, 3, 5, 2, 6, 1, 7, 0):
        z2 = lax.rem(my_z + step, 8) * 2
        rows += [z2 + 1 - core, z2 + core]
    rows = [(r, r * 8) for r in rows]

    def far(j):
        return 2 + (1 - 2 * lax.rem(j, 2)) * ((j + 1) // 2)

    def for_column(i, j, step, count=ROWS):
        y, x = lax.rem(my_y + FAR[i], 4), lax.rem(my_x + far(j), 4)
        first, part = (y * 4 + x) * ROWS, lax.rem(x, 2) * 128 + y * 2 + x // 2
        for r, r8 in rows[:count]:
            step(i, first + r, part + r8)

    def for_quarter(i, step):
        def one(j, carry):
            for_column(i, j, step)
            return carry

        if i < 3:
            lax.fori_loop(0, 4, one, 0)
        else:
            lax.fori_loop(0, 3, one, 0)
            for_column(3, 3, step, ROWS - 1)

    def for_all_peers(step):
        for i in range(4):
            for_quarter(i, step)

    barrier = pltpu.get_barrier_semaphore()

    def greet(i, there, device):
        pl.semaphore_signal(barrier, inc=1, device_id=device, device_id_type=LOGICAL)


    size = 2 * DEVICES
    pairs = (
        (noise_h, noise), (source_h, source),
        (wide_h.at[pl.ds(0, 2 * size)], wide.at[pl.ds(0, 2 * size)]),
        (narrow_h, narrow), (tables_h, tables_v),
        (wide_h.at[pl.ds(2 * size, 4 * size)], wide.at[pl.ds(2 * size, 4 * size)]),
    )
    loads = [pltpu.make_async_copy(a, b, table_sem.at[i]) for i, (a, b) in enumerate(pairs)]
    for load in loads[:3]:
        load.start()
    for_all_peers(greet)
    for load in loads[3:]:
        load.start()

    class Parts:
        def __init__(self, ref, at, count):
            self.ref, self.at, self.count = ref, at, count

        def __getitem__(self, part):
            return self.ref[pl.ds(self.at + part * self.count, self.count)]

    third_t = Parts(wide, 0, size)
    inner, inner_t, inner_c, coarse_third = (Parts(narrow, i * size, DEVICES) for i in range(4))
    twist, twist_c, waves = (tables_v.at[0], tables_v.at[1]), (tables_v.at[2], tables_v.at[3]), tables_v.at[pl.ds(4, 3)]

    for ref, width in ((ke, QB), (fe, QB), (fc, half_q)):
        for at in (0, EDGE + width):
            ref[:, pl.ds(at, EDGE)] = jnp.zeros((ref.shape[0], EDGE, ref.shape[2]), F32)

    for edge, last in ((0, False), (ROWS - 1, True)):

        @pl.when(row == edge)
        def _(last=last):
            for ref, width, layers in ((ke, QB, 2), (fe, QB, 1), (fc, half_q, 1)):
                at = ref.shape[0] - layers if last else 0
                ref[pl.ds(at, layers), pl.ds(EDGE, width)] = jnp.zeros((layers, width, ref.shape[2]), F32)

    loads[0].wait()
    loads[1].wait()
    loads[2].wait()
    noise_rows = noise[...].reshape(LANES, N2)
    contract = (((1,), (1,)), ((), ()))
    spectrum = lax.dot_general(third_t[0], noise_rows, contract, preferred_element_type=F32)
    spectrum = spectrum + lax.dot_general(third_t[1], noise_rows, contract, preferred_element_type=F32)
    send_f[...] = spectrum.reshape(DEVICES, 2, LANES)

    fe[pl.ds(1, PB), pl.ds(EDGE, QB)] = source[...].astype(F32)
    scol_s[0, :, 0] = fe[pl.ds(1, PB), EDGE]
    scol_s[1, :, 0] = fe[pl.ds(1, PB), EDGE + QB - 1]

    pl.semaphore_wait(barrier, DEVICES - 1)

    def push(i, there, device):
        pltpu.make_async_remote_copy(
            src_ref=send_f.at[there], dst_ref=recv_f.at[place], send_sem=fwd_s, recv_sem=fwd_r.at[i],
            device_id=device, device_id_type=LOGICAL,
        ).start()

    for_all_peers(push)
    recv_f[place] = send_f[place]

    loads[3].wait()
    loads[4].wait()
    high, low = halves(dot(narrow[pl.ds(5 * size, 32), pl.ds(0, LANES)], source[...].reshape(LANES, N2)))
    pool = narrow[pl.ds(4 * size, size)]
    pooled = (dot(high, pool) + dot(low, pool)).reshape(half_p, half_q, half_n)
    fc[pl.ds(1, half_p), pl.ds(EDGE, half_q)] = pooled
    cscol_s[0, :, 0] = pooled[:, 0]
    cscol_s[1, :, 0] = pooled[:, half_q - 1]

    def neighbour(d):
        dr, dc = DIRECTIONS[d]
        r, c = row + dr, group + dc
        exists = (r >= 0) & (r < ROWS) & (c >= 0) & (c < COLS)
        return exists, flat_id(r, c)

    mid, mid_c = pl.ds(EDGE, QB), pl.ds(EDGE, half_q)

    def halo_copy(d, kind):
        back = OPPOSITE[d]
        if kind == "source":
            if d < 2:
                return (
                    fe.at[1 if d == 0 else PB, mid], fe.at[PB + 1 if d == 0 else 0, mid],
                    fe.at[0 if d == 0 else PB + 1, mid], src_s, src_r,
                )
            return scol_s.at[d - 2], scol_r.at[back - 2], scol_r.at[d - 2], src_s, src_r
        if kind == "coarse":
            if d < 2:
                return (
                    fc.at[1 if d == 0 else half_p, mid_c], fc.at[half_p + 1 if d == 0 else 0, mid_c],
                    fc.at[0 if d == 0 else half_p + 1, mid_c], csrc_s, csrc_r,
                )
            return cscol_s.at[d - 2], cscol_r.at[back - 2], cscol_r.at[d - 2], csrc_s, csrc_r
        if d < 2:
            return (
                ke.at[pl.ds(2 if d == 0 else PB, 2), mid], ke.at[pl.ds(PB + 2 if d == 0 else 0, 2), mid],
                ke.at[pl.ds(0 if d == 0 else PB + 2, 2), mid], halo_s, halo_r,
            )
        if d < 4:
            return col_s.at[d - 2], col_r.at[back - 2], col_r.at[d - 2], halo_s, halo_r
        return cor_s.at[d - 4], cor_r.at[back - 4], cor_r.at[d - 4], halo_s, halo_r

    def halo_start(d, kind):
        exists, there = neighbour(d)
        src, dst, _, s_sem, r_sem = halo_copy(d, kind)

        @pl.when(exists)
        def _():
            pltpu.make_async_remote_copy(
                src_ref=src, dst_ref=dst, send_sem=s_sem.at[d], recv_sem=r_sem.at[OPPOSITE[d]], device_id=there,
                device_id_type=LOGICAL,
            ).start()

    def halo_wait(d, kind, then):
        exists, there = neighbour(d)
        src, _, here, s_sem, r_sem = halo_copy(d, kind)

        @pl.when(exists)
        def _():
            copy = pltpu.make_async_remote_copy(
                src_ref=src, dst_ref=here, send_sem=s_sem.at[d], recv_sem=r_sem.at[d], device_id=there,
                device_id_type=LOGICAL,
            )
            copy.wait_send()
            copy.wait_recv()
            then(d)

    for d in range(4):
        halo_start(d, "source")
        halo_start(d, "coarse")

    third = core * 128 + place // 2
    third_f = third.astype(F32)
    weight = jnp.where(third == 0, 1.0, 2.0)
    damp = weight / (1.0 + (2.0 * math.pi * CORRELATION) ** 2 * (waves[0] + third_f * third_f))
    amp = waves[1] * damp
    amp_c = waves[2] * damp
    loads[5].wait()

    def copies_of(send, got, s_sem, r_sem, count):
        some = pl.ds(0, count)
        return pltpu.make_async_remote_copy(
            src_ref=send.at[some], dst_ref=got.at[some], send_sem=s_sem, recv_sem=r_sem, device_id=me,
            device_id_type=LOGICAL,
        )

    z = None
    for i in range(4):
        copies_of(send_f, recv_f, fwd_s, fwd_r.at[i], 64 if i < 3 else 63).wait_recv()
        y4 = lax.rem(my_y + 4 - FAR[i], 4)
        columns = pl.ds(pl.multiple_of(y4 * LANES, LANES), LANES)
        high, low = halves(recv_f[pl.ds(y4 * 64, 64)].reshape(LANES, LANES))
        both = dot(wide[pl.ds(2 * size, size), columns], jnp.concatenate([high, low], axis=1))
        term = both[:, :LANES] + (both[:, LANES:] + dot(wide[pl.ds(3 * size, size), columns], high))
        z = term if z is None else z + term
    z_re, z_im = z[:DEVICES], z[DEVICES:]
    cos, sin = twist[0][...], twist[1][...]
    turned = jnp.concatenate([z_re * cos + z_im * sin, z_im * cos - z_re * sin], axis=1)
    y = table_right(turned, inner)
    x = table_right(y * jnp.concatenate([amp, amp], axis=1), inner_t)
    x_re, x_im = x[:, :LANES], x[:, LANES:]
    fine_part = jnp.concatenate([x_re * cos - x_im * sin, x_im * cos + x_re * sin], axis=0)
    high, low = halves(fine_part)
    high_low = jnp.concatenate([high, low], axis=1)

    def push_back(i, there, device):
        pltpu.make_async_remote_copy(
            src_ref=send_i.at[there], dst_ref=recv_i.at[place], send_sem=inv_s, recv_sem=inv_r.at[i],
            device_id=device, device_id_type=LOGICAL,
        ).start()

    coarse_place = place // 2

    def push_coarse(i, there, device):
        pltpu.make_async_remote_copy(
            src_ref=send_c.at[there], dst_ref=recv_c.at[coarse_place], send_sem=crs_sem.at[0],
            recv_sem=crs_sem.at[1], device_id=device, device_id_type=LOGICAL,
        ).start()

    for i in range(4):
        y4 = lax.rem(my_y + FAR[i], 4)
        upper = wide[pl.ds(4 * size + y4 * LANES, LANES)]
        lower = wide[pl.ds(5 * size + y4 * LANES, LANES)]
        both = dot(upper, high_low)
        planes = both[:, :LANES] + (both[:, LANES:] + dot(lower, high))
        send_i[pl.ds(y4 * 64, 64)] = planes.reshape(64, 2, LANES)
        for_quarter(i, push_back)
    recv_i[place] = send_i[place]

    @pl.when(core == 0)
    def _():
        xc = table_right(y * jnp.concatenate([amp_c, amp_c], axis=1), inner_c)
        xc_re, xc_im = xc[:, :LANES], xc[:, LANES:]
        cos_c, sin_c = twist_c[0][...], twist_c[1][...]
        high, low = halves(jnp.concatenate([xc_re * cos_c - xc_im * sin_c, xc_im * cos_c + xc_re * sin_c], axis=0))
        high_low = jnp.concatenate([high, low], axis=1)
        for i in range(4):
            y4 = lax.rem(my_y + FAR[i], 4)
            upper = wide[pl.ds(4 * size + y4 * LANES, LANES)]
            lower = wide[pl.ds(5 * size + y4 * LANES, LANES)]
            both = dot(upper, high_low)
            planes = both[:, :LANES] + (both[:, LANES:] + dot(lower, high))
            send_c[pl.ds(y4 * 64, 64)] = planes.reshape(64, 2, LANES)
            for_quarter(i, push_coarse)
        recv_c[coarse_place] = send_c[place]

    def put_source(d):
        if d >= 2:
            at = EDGE - 1 if d == 2 else EDGE + QB
            for plane in range(PB):
                fe[1 + plane, pl.ds(at, 1)] = scol_r[d - 2, plane]

    def put_coarse(d):
        if d >= 2:
            at = EDGE - 1 if d == 2 else EDGE + half_q
            for plane in range(half_p):
                fc[1 + plane, pl.ds(at, 1)] = cscol_r[d - 2, plane]

    def put_kappa(d):
        dr, dc = DIRECTIONS[d]
        if d >= 4:
            ke[1 if dr < 0 else PB + 2, pl.ds(EDGE - 1 if dc < 0 else EDGE + QB, 1)] = cor_r[d - 4]
        elif d >= 2:
            at = EDGE - 2 if d == 2 else EDGE + QB
            for plane in range(PB):
                ke[2 + plane, pl.ds(at, 2)] = col_r[d - 2, plane]

    for d in range(4):
        halo_wait(d, "source", put_source)
        halo_wait(d, "coarse", put_coarse)
    copies_of(send_f, recv_f, fwd_s, fwd_r.at[0], DEVICES - 1).wait_send()

    fine_log = None
    for i in range(4):
        copies_of(send_i, recv_i, inv_s, inv_r.at[i], 64 if i < 3 else 63).wait_recv()
        y4 = lax.rem(my_y + 4 - FAR[i], 4)
        high, low = halves(recv_i[pl.ds(y4 * 64, 64)].reshape(LANES, LANES).T)
        upper, lower = wide[pl.ds(y4 * LANES, LANES)], wide[pl.ds(size + y4 * LANES, LANES)]
        both = dot(jnp.concatenate([high, low], axis=0), upper)
        term = both[:LANES] + (both[LANES:] + dot(high, lower))
        fine_log = term if fine_log is None else fine_log + term
    fine_half = (0.5 * jnp.exp(fine_log)).reshape(PB, QB, N2)
    for i, (dr, dc) in enumerate(DIRECTIONS[4:]):
        cor_s[i, 0] = fine_half[0 if dr < 0 else PB - 1, 0 if dc < 0 else QB - 1]
    col_s[0] = fine_half[:, 0:2]
    col_s[1] = fine_half[:, QB - 2 : QB]
    ke[pl.ds(2, PB), mid] = fine_half
    for d in (4, 5, 6, 7, 2, 3, 0, 1):
        halo_start(d, "kappa")

    for own in range(2):

        @pl.when(core == own)
        def _(own=own):
            copies_of(recv_c, recv_c, crs_sem.at[0], crs_sem.at[1], 127 + own).wait_recv()

    coarse_log = table_right(recv_c[...].reshape(DEVICES, LANES).T, coarse_third)
    cell = lax.broadcasted_iota(jnp.int32, (LANES, half_n), 0)
    n0 = row * half_p + lax.div(cell, CQ) - 2
    n1 = group * half_q + lax.rem(cell, CQ) - 2
    inside = (n0 >= 0) & (n0 < N0 // 2) & (n1 >= 0) & (n1 < N1 // 2)
    coarse_half = jnp.where(inside, 0.5 * jnp.exp(coarse_log), 0.0)
    for plane in range(CP):
        kc[plane, pl.ds(EDGE - 2, CQ)] = coarse_half[plane * CQ : (plane + 1) * CQ]
    smooth(kc, fc, uc, coarse_out, half_p, half_q)

    for d in (0, 1, 2, 3, 4, 5, 6, 7):
        halo_wait(d, "kappa", put_kappa)
    smooth(ke, fe, ue, fine_out, PB, QB)

    copies_of(send_i, recv_i, inv_s, inv_r.at[0], DEVICES - 1).wait_send()

    @pl.when(core == 0)
    def _():
        copies_of(send_c, send_c, crs_sem.at[0], crs_sem.at[1], DEVICES - 1).wait_send()


def hand_over(fine, coarse, fine_out, coarse_out):
    fine_out[...] = fine[...]
    coarse_out[...] = coarse[...]


def body(noise, source):
    constants = tables()
    vmem, anywhere = pl.BlockSpec(memory_space=pltpu.VMEM), pl.BlockSpec(memory_space=pl.ANY)
    half_p, half_q, half_n = PB // 2, QB // 2, N2 // 2
    message = pltpu.VMEM((DEVICES, 2, LANES), F32)
    sems = pltpu.SemaphoreType.DMA
    pressures = pl.pallas_call(
        kernel,
        out_shape=(pltpu.VMEM((PB, QB, N2), F32), pltpu.VMEM((half_p, half_q, half_n), F32)),
        in_specs=[anywhere] * 5,
        out_specs=(vmem, vmem),
        scratch_shapes=[pltpu.VMEM((PB, QB, N2), BF16)] * 2
        + [pltpu.VMEM(table.shape, table.dtype) for table in constants]
        + [message] * 5
        + [pltpu.VMEM((128, 2, LANES), F32)]
        + [
            pltpu.VMEM((PB + 4, QB + 16, N2), F32), pltpu.VMEM((PB + 2, QB + 16, N2), F32),
            pltpu.VMEM((PB + 2, QB + 16, N2), F32),
            pltpu.VMEM((half_p + 4, half_q + 16, half_n), F32), pltpu.VMEM((half_p + 2, half_q + 16, half_n), F32),
            pltpu.VMEM((half_p + 2, half_q + 16, half_n), F32),
        ]
        + [pltpu.VMEM((2, PB, 2, N2), F32)] * 2
        + [pltpu.VMEM((4, 1, N2), F32)] * 2
        + [pltpu.VMEM((2, PB, 1, N2), F32)] * 2
        + [pltpu.VMEM((2, half_p, 1, half_n), F32)] * 2
        + [sems((6,)), sems, sems((4,)), sems, sems((4,)), sems((2,))]
        + [sems((8,))] * 2
        + [sems((4,))] * 4,
        compiler_params=pltpu.CompilerParams(collective_id=0, has_side_effects=True, vmem_limit_bytes=VMEM_LIMIT),
    )(noise, source, *[jnp.asarray(table) for table in constants])
    return pl.pallas_call(
        hand_over,
        out_shape=tuple(jax.ShapeDtypeStruct(value.shape, value.dtype) for value in pressures),
        in_specs=[vmem] * 2,
        out_specs=(vmem, vmem),
        compiler_params=pltpu.CompilerParams(vmem_limit_bytes=2 << 20),
    )(*pressures)


def solution(mesh):
    return jax.shard_map(
        body,
        mesh=mesh,
        in_specs=(P("row", ("level", "col"), None), P("row", ("level", "col"), None)),
        out_specs=(P("row", ("level", "col"), None), P("row", ("level", "col"), None)),
        check_vma=False,
    )
```

```python
import functools
import math

import jax
import jax.numpy as jnp
import ml_dtypes
import numpy as np
from jax import lax
from jax.experimental import pallas as pl
from jax.experimental.pallas import tpu as pltpu
from jax.sharding import PartitionSpec as P

JACOBI_WEIGHT = 2.0 / 3.0
CORRELATION = 0.2
FIELD_SCALE = 0.3
LOGICAL = pl.DeviceIdType.LOGICAL
F32 = jnp.float32
BF16 = jnp.bfloat16

N0, N1, N2 = 64, 512, 512
ROWS, COLS = 16, 16
DEVICES = ROWS * COLS
PB, QB = N0 // ROWS, N1 // COLS
LANES = PB * QB
CP, CQ = PB // 2 + 4, QB // 2 + 4
CELLS = CP * CQ
VMEM_LIMIT = 60 << 20
FAR = (2, 1, 3, 0)
EDGE = 8


def split_table(table):
    high = table.astype(ml_dtypes.bfloat16)
    low = (table - high.astype(np.float64)).astype(ml_dtypes.bfloat16)
    return high, low


def signed(index, length):
    return np.where(index < length // 2, index, index - length).astype(np.float64)


def columns_of(column):
    y, x = column // 4, column % 4
    return (x % 2) * 8 + y * 2 + x // 2


@functools.lru_cache(maxsize=None)
def tables():
    place = np.arange(DEVICES)
    r, c = place % ROWS, columns_of(place // ROWS)
    third = (r % 2) * 128 + place // 2
    turn = 2.0 * np.pi
    n2 = np.arange(N2)
    angle = turn * ((third[:, None] * n2[None, :]) % N2) / N2
    third_table = np.stack([np.cos(angle), -np.sin(angle)], axis=1).reshape(2 * DEVICES, N2)
    k2 = np.arange(128)
    angle = turn * ((k2[:, None] * np.arange(N2 // 2)[None, :]) % (N2 // 2)) / (N2 // 2)
    coarse_third = np.stack([np.cos(angle), -np.sin(angle)], axis=1).reshape(256, N2 // 2)
    a, b = place // 16, place % 16
    angle = turn * ((a[:, None] * r[None, :] + b[:, None] * c[None, :]) % 16) / 16
    cos, sin = np.cos(angle), np.sin(angle)
    outer = np.concatenate([np.stack([cos, sin], axis=2), np.stack([-sin, cos], axis=2)], axis=0)
    outer = outer.reshape(2 * DEVICES, 2 * DEVICES)
    lane = np.arange(LANES)
    p, q = lane // QB, lane % QB
    angle = turn * (((8 * p[:, None] * p[None, :]) + q[:, None] * q[None, :]) % 32) / 32
    cos, sin = np.cos(angle), np.sin(angle)
    inner = np.block([[cos, -sin], [sin, cos]])
    lane_c = np.arange(CELLS)
    pc, qc = lane_c // CQ - 2, lane_c % CQ - 2
    angle = turn * (((8 * p[:, None] * pc[None, :]) + q[:, None] * qc[None, :]) % 16) / 16
    cos, sin = np.cos(angle), np.sin(angle)
    empty = np.zeros((LANES, LANES - CELLS))
    inner_c = np.block([[cos, empty, sin, empty], [-sin, empty, cos, empty]])
    angle = turn * ((8 * a[:, None] * p[None, :] + b[:, None] * q[None, :]) % 512) / 512
    twist = np.stack([np.cos(angle), np.sin(angle)])
    angle = turn * ((8 * a[:, None] * pc[None, :] + b[:, None] * qc[None, :]) % 256) / 256
    rest = np.zeros((DEVICES, LANES - CELLS))
    twist_c = np.stack([np.concatenate([np.cos(angle), rest], 1), np.concatenate([np.sin(angle), rest], 1)])
    m0 = signed(a[:, None] + 16 * p[None, :], N0)
    m1 = signed(b[:, None] + 16 * q[None, :], N1)
    norm = (float(N0) * N1 * N2) ** -0.5
    inside = (m0 != -N0 // 2) & (m1 != -N1 // 2)
    inside_c = (np.abs(m0) < N0 // 4) & (np.abs(m1) < N1 // 4)
    waves = np.stack([m0 * m0 + m1 * m1, inside * FIELD_SCALE * norm, inside_c * FIELD_SCALE * norm])
    pool = (np.arange(N2)[:, None] // 2 == np.arange(N2 // 2)[None, :]).astype(ml_dtypes.bfloat16)
    pool_rows = (np.arange(32)[:, None] == ((p // 2) * 16 + q // 2)[None, :]) * 0.125
    pool_rows = np.concatenate([pool_rows, np.zeros((32, LANES))], axis=1).astype(ml_dtypes.bfloat16)
    wide = np.concatenate([part for table in (third_table, outer, outer.T) for part in split_table(table)])
    narrow = np.concatenate([part for table in (inner, inner.T, inner_c, coarse_third) for part in split_table(table)])
    narrow = np.concatenate([narrow, pool, pool_rows])
    return wide, narrow, np.concatenate([twist, twist_c, waves]).astype(np.float32)


def halves(value):
    high = value.astype(BF16)
    return high, (value - high.astype(F32)).astype(BF16)


def dot(left, right):
    return jnp.dot(left, right, preferred_element_type=F32)


def table_right(value, table):
    high, low = halves(value)
    return dot(high, table[0]) + (dot(high, table[1]) + dot(low, table[0]))


DIRECTIONS = ((-1, 0), (1, 0), (0, -1), (0, 1), (-1, -1), (-1, 1), (1, -1), (1, 1))
OPPOSITE = (1, 0, 3, 2, 7, 6, 5, 4)


def flat_id(r, c):
    return (c // 8) * 128 + r * 8 + c % 8


def beside_lanes(value):
    depth = value.shape[-1]
    lane = lax.broadcasted_iota(jnp.int32, value.shape, 1)
    after = jnp.where(lane == depth - 1, 0.0, pltpu.roll(value, depth - 1, 1))
    before = jnp.where(lane == 0, 0.0, pltpu.roll(value, 1, 1))
    return after, before


def first_sweep(half, neighbours, source):
    diagonal = 6.0 * half
    for beside in neighbours:
        diagonal = diagonal + jnp.where(beside > 0.0, beside, half)
    rate = JACOBI_WEIGHT / diagonal
    return source * jnp.where(half > 0.0, rate, JACOBI_WEIGHT), diagonal, rate


def smooth(halved, source, first, rates, out, planes, width):
    mid, low, high = pl.ds(EDGE, width), pl.ds(EDGE - 1, width), pl.ds(EDGE + 1, width)
    for plane in range(planes + 2):
        half = halved[plane + 1, mid]
        near = (halved[plane + 2, mid], halved[plane, mid], halved[plane + 1, high], halved[plane + 1, low])
        value, diagonal, rate = first_sweep(half, near + beside_lanes(half), source[plane, mid])
        first[plane, mid] = value
        if 1 <= plane <= planes:
            out[plane - 1] = diagonal
            rates[plane - 1] = rate
    for at, inward, outward in ((EDGE - 1, EDGE, EDGE - 2), (EDGE + width, EDGE + width - 1, EDGE + width + 1)):

        def line(ref, base, q):
            return jnp.concatenate([ref[base + plane, pl.ds(q, 1)] for plane in range(planes)], axis=0)

        half = line(halved, 2, at)
        near = (line(halved, 3, at), line(halved, 1, at), line(halved, 2, inward), line(halved, 2, outward))
        value, _, _ = first_sweep(half, near + beside_lanes(half), line(source, 1, at))
        for plane in range(planes):
            first[1 + plane, pl.ds(at, 1)] = value[plane : plane + 1]
    for plane in range(planes):
        half = halved[plane + 2, mid]
        inner = first[plane + 1, mid]
        diagonal = out[plane]
        total = source[plane + 1, mid] - diagonal * inner
        after, before = beside_lanes(half)
        after_value, before_value = beside_lanes(inner)
        for beside, value in (
            (halved[plane + 3, mid], first[plane + 2, mid]),
            (halved[plane + 1, mid], first[plane, mid]),
            (halved[plane + 2, high], first[plane + 1, high]),
            (halved[plane + 2, low], first[plane + 1, low]),
            (after, after_value),
            (before, before_value),
        ):
            total = total + (half + jnp.where(beside > 0.0, beside, half)) * value
        out[plane] = inner + total * rates[plane]


def kernel(
    noise_h, source_h, wide_h, narrow_h, tables_h, fine_out, coarse_out,
    noise, source, wide, narrow, tables_v,
    send_f, recv_f, send_i, recv_i, send_c, recv_c,
    ke, fe, ue, kc, fc, uc, re, rc,
    col_s, col_r, cor_s, cor_r, scol_s, scol_r, cscol_s, cscol_r,
    table_sem, fwd_s, fwd_r, inv_s, inv_r, crs_sem, halo_s, halo_r, src_s, src_r, csrc_s, csrc_r,
):
    level, row, col = lax.axis_index("level"), lax.axis_index("row"), lax.axis_index("col")
    group = level * 8 + col
    me = flat_id(row, group)
    core, my_z = lax.rem(row, 2), row // 2
    my_y, my_x = col // 2, lax.rem(col, 2) * 2 + level
    place = (my_y * 4 + my_x) * ROWS + row
    half_p, half_q, half_n = PB // 2, QB // 2, N2 // 2

    rows = []
    for step in (4, 3, 5, 2, 6, 1, 7, 0):
        z2 = lax.rem(my_z + step, 8) * 2
        rows += [z2 + 1 - core, z2 + core]
    rows = [(r, r * 8) for r in rows]

    def far(j):
        return 2 + (1 - 2 * lax.rem(j, 2)) * ((j + 1) // 2)

    def for_column(i, j, step, count=ROWS):
        y, x = lax.rem(my_y + FAR[i], 4), lax.rem(my_x + far(j), 4)
        first, part = (y * 4 + x) * ROWS, lax.rem(x, 2) * 128 + y * 2 + x // 2
        for r, r8 in rows[:count]:
            step(i, first + r, part + r8)

    def for_quarter(i, step):
        def one(j, carry):
            for_column(i, j, step)
            return carry

        if i < 3:
            lax.fori_loop(0, 4, one, 0)
        else:
            lax.fori_loop(0, 3, one, 0)
            for_column(3, 3, step, ROWS - 1)

    def for_all_peers(step):
        for i in range(4):
            for_quarter(i, step)

    barrier = pltpu.get_barrier_semaphore()

    def greet(i, there, device):
        pl.semaphore_signal(barrier, inc=1, device_id=device, device_id_type=LOGICAL)


    size = 2 * DEVICES
    pairs = (
        (noise_h, noise), (source_h, source),
        (wide_h.at[pl.ds(0, 2 * size)], wide.at[pl.ds(0, 2 * size)]),
        (narrow_h, narrow), (tables_h, tables_v),
        (wide_h.at[pl.ds(2 * size, 4 * size)], wide.at[pl.ds(2 * size, 4 * size)]),
    )
    loads = [pltpu.make_async_copy(a, b, table_sem.at[i]) for i, (a, b) in enumerate(pairs)]
    for load in loads[:3]:
        load.start()
    for_all_peers(greet)
    for load in loads[3:]:
        load.start()

    class Parts:
        def __init__(self, ref, at, count):
            self.ref, self.at, self.count = ref, at, count

        def __getitem__(self, part):
            return self.ref[pl.ds(self.at + part * self.count, self.count)]

    third_t = Parts(wide, 0, size)
    inner, inner_t, inner_c, coarse_third = (Parts(narrow, i * size, DEVICES) for i in range(4))
    twist, twist_c, waves = (tables_v.at[0], tables_v.at[1]), (tables_v.at[2], tables_v.at[3]), tables_v.at[pl.ds(4, 3)]

    for ref, width in ((ke, QB), (fe, QB), (fc, half_q)):
        for at in (0, EDGE + width):
            ref[:, pl.ds(at, EDGE)] = jnp.zeros((ref.shape[0], EDGE, ref.shape[2]), F32)

    for edge, last in ((0, False), (ROWS - 1, True)):

        @pl.when(row == edge)
        def _(last=last):
            for ref, width, layers in ((ke, QB, 2), (fe, QB, 1), (fc, half_q, 1)):
                at = ref.shape[0] - layers if last else 0
                ref[pl.ds(at, layers), pl.ds(EDGE, width)] = jnp.zeros((layers, width, ref.shape[2]), F32)

    loads[0].wait()
    loads[1].wait()
    loads[2].wait()
    noise_rows = noise[...].reshape(LANES, N2)
    contract = (((1,), (1,)), ((), ()))
    spectrum = lax.dot_general(third_t[0], noise_rows, contract, preferred_element_type=F32)
    spectrum = spectrum + lax.dot_general(third_t[1], noise_rows, contract, preferred_element_type=F32)
    send_f[...] = spectrum.reshape(DEVICES, 2, LANES)

    fe[pl.ds(1, PB), pl.ds(EDGE, QB)] = source[...].astype(F32)
    scol_s[0, :, 0] = fe[pl.ds(1, PB), EDGE]
    scol_s[1, :, 0] = fe[pl.ds(1, PB), EDGE + QB - 1]

    pl.semaphore_wait(barrier, DEVICES - 1)

    def push(i, there, device):
        pltpu.make_async_remote_copy(
            src_ref=send_f.at[there], dst_ref=recv_f.at[place], send_sem=fwd_s, recv_sem=fwd_r.at[i],
            device_id=device, device_id_type=LOGICAL,
        ).start()

    for_all_peers(push)
    recv_f[place] = send_f[place]

    loads[3].wait()
    loads[4].wait()
    high, low = halves(dot(narrow[pl.ds(5 * size, 32), pl.ds(0, LANES)], source[...].reshape(LANES, N2)))
    pool = narrow[pl.ds(4 * size, size)]
    pooled = (dot(high, pool) + dot(low, pool)).reshape(half_p, half_q, half_n)
    fc[pl.ds(1, half_p), pl.ds(EDGE, half_q)] = pooled
    cscol_s[0, :, 0] = pooled[:, 0]
    cscol_s[1, :, 0] = pooled[:, half_q - 1]

    def neighbour(d):
        dr, dc = DIRECTIONS[d]
        r, c = row + dr, group + dc
        exists = (r >= 0) & (r < ROWS) & (c >= 0) & (c < COLS)
        return exists, flat_id(r, c)

    mid, mid_c = pl.ds(EDGE, QB), pl.ds(EDGE, half_q)

    def halo_copy(d, kind):
        back = OPPOSITE[d]
        if kind == "source":
            if d < 2:
                return (
                    fe.at[1 if d == 0 else PB, mid], fe.at[PB + 1 if d == 0 else 0, mid],
                    fe.at[0 if d == 0 else PB + 1, mid], src_s, src_r,
                )
            return scol_s.at[d - 2], scol_r.at[back - 2], scol_r.at[d - 2], src_s, src_r
        if kind == "coarse":
            if d < 2:
                return (
                    fc.at[1 if d == 0 else half_p, mid_c], fc.at[half_p + 1 if d == 0 else 0, mid_c],
                    fc.at[0 if d == 0 else half_p + 1, mid_c], csrc_s, csrc_r,
                )
            return cscol_s.at[d - 2], cscol_r.at[back - 2], cscol_r.at[d - 2], csrc_s, csrc_r
        if d < 2:
            return (
                ke.at[pl.ds(2 if d == 0 else PB, 2), mid], ke.at[pl.ds(PB + 2 if d == 0 else 0, 2), mid],
                ke.at[pl.ds(0 if d == 0 else PB + 2, 2), mid], halo_s, halo_r,
            )
        if d < 4:
            return col_s.at[d - 2], col_r.at[back - 2], col_r.at[d - 2], halo_s, halo_r
        return cor_s.at[d - 4], cor_r.at[back - 4], cor_r.at[d - 4], halo_s, halo_r

    def halo_start(d, kind):
        exists, there = neighbour(d)
        src, dst, _, s_sem, r_sem = halo_copy(d, kind)

        @pl.when(exists)
        def _():
            pltpu.make_async_remote_copy(
                src_ref=src, dst_ref=dst, send_sem=s_sem.at[d], recv_sem=r_sem.at[OPPOSITE[d]], device_id=there,
                device_id_type=LOGICAL,
            ).start()

    def halo_wait(d, kind, then):
        exists, there = neighbour(d)
        src, _, here, s_sem, r_sem = halo_copy(d, kind)

        @pl.when(exists)
        def _():
            copy = pltpu.make_async_remote_copy(
                src_ref=src, dst_ref=here, send_sem=s_sem.at[d], recv_sem=r_sem.at[d], device_id=there,
                device_id_type=LOGICAL,
            )
            copy.wait_send()
            copy.wait_recv()
            then(d)

    for d in range(4):
        halo_start(d, "source")
        halo_start(d, "coarse")

    third = core * 128 + place // 2
    third_f = third.astype(F32)
    weight = jnp.where(third == 0, 1.0, 2.0)
    damp = weight / (1.0 + (2.0 * math.pi * CORRELATION) ** 2 * (waves[0] + third_f * third_f))
    amp = waves[1] * damp
    amp_c = waves[2] * damp
    loads[5].wait()

    def copies_of(send, got, s_sem, r_sem, count):
        some = pl.ds(0, count)
        return pltpu.make_async_remote_copy(
            src_ref=send.at[some], dst_ref=got.at[some], send_sem=s_sem, recv_sem=r_sem, device_id=me,
            device_id_type=LOGICAL,
        )

    z = None
    for i in range(4):
        copies_of(send_f, recv_f, fwd_s, fwd_r.at[i], 64 if i < 3 else 63).wait_recv()
        y4 = lax.rem(my_y + 4 - FAR[i], 4)
        columns = pl.ds(pl.multiple_of(y4 * LANES, LANES), LANES)
        high, low = halves(recv_f[pl.ds(y4 * 64, 64)].reshape(LANES, LANES))
        both = dot(wide[pl.ds(2 * size, size), columns], jnp.concatenate([high, low], axis=1))
        term = both[:, :LANES] + (both[:, LANES:] + dot(wide[pl.ds(3 * size, size), columns], high))
        z = term if z is None else z + term
    z_re, z_im = z[:DEVICES], z[DEVICES:]
    cos, sin = twist[0][...], twist[1][...]
    turned = jnp.concatenate([z_re * cos + z_im * sin, z_im * cos - z_re * sin], axis=1)
    y = table_right(turned, inner)
    x = table_right(y * jnp.concatenate([amp, amp], axis=1), inner_t)
    x_re, x_im = x[:, :LANES], x[:, LANES:]
    fine_part = jnp.concatenate([x_re * cos - x_im * sin, x_im * cos + x_re * sin], axis=0)
    high, low = halves(fine_part)
    high_low = jnp.concatenate([high, low], axis=1)

    def push_back(i, there, device):
        pltpu.make_async_remote_copy(
            src_ref=send_i.at[there], dst_ref=recv_i.at[place], send_sem=inv_s, recv_sem=inv_r.at[i],
            device_id=device, device_id_type=LOGICAL,
        ).start()

    coarse_place = place // 2

    def push_coarse(i, there, device):
        pltpu.make_async_remote_copy(
            src_ref=send_c.at[there], dst_ref=recv_c.at[coarse_place], send_sem=crs_sem.at[0],
            recv_sem=crs_sem.at[1], device_id=device, device_id_type=LOGICAL,
        ).start()

    for i in range(4):
        y4 = lax.rem(my_y + FAR[i], 4)
        upper = wide[pl.ds(4 * size + y4 * LANES, LANES)]
        lower = wide[pl.ds(5 * size + y4 * LANES, LANES)]
        both = dot(upper, high_low)
        planes = both[:, :LANES] + (both[:, LANES:] + dot(lower, high))
        send_i[pl.ds(y4 * 64, 64)] = planes.reshape(64, 2, LANES)
        for_quarter(i, push_back)
    recv_i[place] = send_i[place]

    @pl.when(core == 0)
    def _():
        xc = table_right(y * jnp.concatenate([amp_c, amp_c], axis=1), inner_c)
        xc_re, xc_im = xc[:, :LANES], xc[:, LANES:]
        cos_c, sin_c = twist_c[0][...], twist_c[1][...]
        high, low = halves(jnp.concatenate([xc_re * cos_c - xc_im * sin_c, xc_im * cos_c + xc_re * sin_c], axis=0))
        high_low = jnp.concatenate([high, low], axis=1)
        for i in range(4):
            y4 = lax.rem(my_y + FAR[i], 4)
            upper = wide[pl.ds(4 * size + y4 * LANES, LANES)]
            lower = wide[pl.ds(5 * size + y4 * LANES, LANES)]
            both = dot(upper, high_low)
            planes = both[:, :LANES] + (both[:, LANES:] + dot(lower, high))
            send_c[pl.ds(y4 * 64, 64)] = planes.reshape(64, 2, LANES)
            for_quarter(i, push_coarse)
        recv_c[coarse_place] = send_c[place]

    def put_source(d):
        if d >= 2:
            at = EDGE - 1 if d == 2 else EDGE + QB
            for plane in range(PB):
                fe[1 + plane, pl.ds(at, 1)] = scol_r[d - 2, plane]

    def put_coarse(d):
        if d >= 2:
            at = EDGE - 1 if d == 2 else EDGE + half_q
            for plane in range(half_p):
                fc[1 + plane, pl.ds(at, 1)] = cscol_r[d - 2, plane]

    def put_kappa(d):
        dr, dc = DIRECTIONS[d]
        if d >= 4:
            ke[1 if dr < 0 else PB + 2, pl.ds(EDGE - 1 if dc < 0 else EDGE + QB, 1)] = cor_r[d - 4]
        elif d >= 2:
            at = EDGE - 2 if d == 2 else EDGE + QB
            for plane in range(PB):
                ke[2 + plane, pl.ds(at, 2)] = col_r[d - 2, plane]

    for d in range(4):
        halo_wait(d, "source", put_source)
        halo_wait(d, "coarse", put_coarse)
    copies_of(send_f, recv_f, fwd_s, fwd_r.at[0], DEVICES - 1).wait_send()

    fine_log = None
    for i in range(4):
        copies_of(send_i, recv_i, inv_s, inv_r.at[i], 64 if i < 3 else 63).wait_recv()
        y4 = lax.rem(my_y + 4 - FAR[i], 4)
        high, low = halves(recv_i[pl.ds(y4 * 64, 64)].reshape(LANES, LANES).T)
        upper, lower = wide[pl.ds(y4 * LANES, LANES)], wide[pl.ds(size + y4 * LANES, LANES)]
        both = dot(jnp.concatenate([high, low], axis=0), upper)
        term = both[:LANES] + (both[LANES:] + dot(high, lower))
        fine_log = term if fine_log is None else fine_log + term
    fine_half = (0.5 * jnp.exp(fine_log)).reshape(PB, QB, N2)
    for i, (dr, dc) in enumerate(DIRECTIONS[4:]):
        cor_s[i, 0] = fine_half[0 if dr < 0 else PB - 1, 0 if dc < 0 else QB - 1]
    col_s[0] = fine_half[:, 0:2]
    col_s[1] = fine_half[:, QB - 2 : QB]
    ke[pl.ds(2, PB), mid] = fine_half
    for d in (4, 5, 6, 7, 2, 3, 0, 1):
        halo_start(d, "kappa")

    for own in range(2):

        @pl.when(core == own)
        def _(own=own):
            copies_of(recv_c, recv_c, crs_sem.at[0], crs_sem.at[1], 127 + own).wait_recv()

    coarse_log = table_right(recv_c[...].reshape(DEVICES, LANES).T, coarse_third)
    cell = lax.broadcasted_iota(jnp.int32, (LANES, half_n), 0)
    n0 = row * half_p + lax.div(cell, CQ) - 2
    n1 = group * half_q + lax.rem(cell, CQ) - 2
    inside = (n0 >= 0) & (n0 < N0 // 2) & (n1 >= 0) & (n1 < N1 // 2)
    coarse_half = jnp.where(inside, 0.5 * jnp.exp(coarse_log), 0.0)
    for plane in range(CP):
        kc[plane, pl.ds(EDGE - 2, CQ)] = coarse_half[plane * CQ : (plane + 1) * CQ]
    smooth(kc, fc, uc, rc, coarse_out, half_p, half_q)

    for d in (0, 1, 2, 3, 4, 5, 6, 7):
        halo_wait(d, "kappa", put_kappa)
    smooth(ke, fe, ue, re, fine_out, PB, QB)

    copies_of(send_i, recv_i, inv_s, inv_r.at[0], DEVICES - 1).wait_send()

    @pl.when(core == 0)
    def _():
        copies_of(send_c, send_c, crs_sem.at[0], crs_sem.at[1], DEVICES - 1).wait_send()


def hand_over(fine, coarse, fine_out, coarse_out):
    fine_out[...] = fine[...]
    coarse_out[...] = coarse[...]


def body(noise, source):
    constants = tables()
    vmem, anywhere = pl.BlockSpec(memory_space=pltpu.VMEM), pl.BlockSpec(memory_space=pl.ANY)
    half_p, half_q, half_n = PB // 2, QB // 2, N2 // 2
    message = pltpu.VMEM((DEVICES, 2, LANES), F32)
    sems = pltpu.SemaphoreType.DMA
    pressures = pl.pallas_call(
        kernel,
        out_shape=(pltpu.VMEM((PB, QB, N2), F32), pltpu.VMEM((half_p, half_q, half_n), F32)),
        in_specs=[anywhere] * 5,
        out_specs=(vmem, vmem),
        scratch_shapes=[pltpu.VMEM((PB, QB, N2), BF16)] * 2
        + [pltpu.VMEM(table.shape, table.dtype) for table in constants]
        + [message] * 5
        + [pltpu.VMEM((128, 2, LANES), F32)]
        + [
            pltpu.VMEM((PB + 4, QB + 16, N2), F32), pltpu.VMEM((PB + 2, QB + 16, N2), F32),
            pltpu.VMEM((PB + 2, QB + 16, N2), F32),
            pltpu.VMEM((half_p + 4, half_q + 16, half_n), F32), pltpu.VMEM((half_p + 2, half_q + 16, half_n), F32),
            pltpu.VMEM((half_p + 2, half_q + 16, half_n), F32),
            pltpu.VMEM((PB, QB, N2), F32), pltpu.VMEM((half_p, half_q, half_n), F32),
        ]
        + [pltpu.VMEM((2, PB, 2, N2), F32)] * 2
        + [pltpu.VMEM((4, 1, N2), F32)] * 2
        + [pltpu.VMEM((2, PB, 1, N2), F32)] * 2
        + [pltpu.VMEM((2, half_p, 1, half_n), F32)] * 2
        + [sems((6,)), sems, sems((4,)), sems, sems((4,)), sems((2,))]
        + [sems((8,))] * 2
        + [sems((4,))] * 4,
        compiler_params=pltpu.CompilerParams(collective_id=0, has_side_effects=True, vmem_limit_bytes=VMEM_LIMIT),
    )(noise, source, *[jnp.asarray(table) for table in constants])
    return pl.pallas_call(
        hand_over,
        out_shape=tuple(jax.ShapeDtypeStruct(value.shape, value.dtype) for value in pressures),
        in_specs=[vmem] * 2,
        out_specs=(vmem, vmem),
        compiler_params=pltpu.CompilerParams(vmem_limit_bytes=2 << 20),
    )(*pressures)


def solution(mesh):
    return jax.shard_map(
        body,
        mesh=mesh,
        in_specs=(P("row", ("level", "col"), None), P("row", ("level", "col"), None)),
        out_specs=(P("row", ("level", "col"), None), P("row", ("level", "col"), None)),
        check_vma=False,
    )
```
